128 devices in a mesh: dp: 16 (over y, x), tensor: 8 (over z, core).
Axes of the slice: x: 4, y: 4, z: 4, core: 2. Of those that a mesh axis runs over, the one named last changes fastest.
Arguments:
- queries: bfloat16 [6144, 8192], P('dp', 'tensor'), may hold values from -16 to 16
- fresh_kv: bfloat16 [6144, 2048], P('dp', 'tensor'), may hold values from -17 to 17
- kv_pool: bfloat16 [720, 64, 2048], P('dp', None, 'tensor'), may hold values from -9 to 9
- page_table: int32 [384, 16], replicated, may hold values from 0 to 719, as said below
- path_len: int32 [384], replicated, may hold values from 769 to 1024, as said below
- parent: int32 [384], replicated, may hold values from -1 to 383, as said below
- w_out: bfloat16 [8192, 8192], P('tensor'), may hold values from -4 to 4
- residual: bfloat16 [6144, 8192], P('dp'), may hold values from -6 to 6
- gain: bfloat16 [8192], replicated, may hold values from 0.5 to 1.5
Outputs:
- mixed: bfloat16 [6144, 8192], P('dp', 'tensor')
- normed: bfloat16 [6144, 8192], P('dp', 'tensor')
The draws below stay inside these ranges and needn't reach their ends.
Inputs may be any that keep to these rules, and one draw needn't show every extreme that they name: `page_table`: page p is held by dp rank p // 45. Each rank's nodes form aligned families of 4 consecutive nodes sharing their first 8 pages; all other entries among one rank's nodes are distinct pages. For every pair of ranks, the nodes of the first reference exactly 24 page slots and exactly 15 distinct pages held by the second. `path_len`: some node's path is full. `parent`: the first 12 nodes of each rank have -1; every other node names one of those nodes, on any rank.
All inputs are finite; a program needn't handle non-finite values.
Results may differ from the reference program's by a relative error of at most 0.019.
Values may be sent and summed in bfloat16 or wider, within the bound.
No kernel may reach another device: no remote copies, remote signals or barrier semaphores. Data moves between devices by JAX's collectives and lax.ppermute only.
A program may use at most 192 MiB of HBM per device.

```python
import jax
import jax.numpy as jnp
from jax import lax

D = 8192
HEADS = 64
KV_HEADS = 8
HD = 128
NODES_DEV = 24
NEW = 16
PAGE = 64
PATH_PAGES = 16
SHARED = 8
FAM = 4
ALL_NODES = 384
TOKENS = 6144
PATH = 1024
P_DEV = 45
PAGES = 720
N_DP = 16
N_TENSOR = 8


def draw_queries(key, part):
    key = jax.random.fold_in(key, 1)
    first = jax.random.fold_in(key, 0)
    group = HEADS // KV_HEADS
    values = jax.random.truncated_normal(first, -6.0, 6.0, (TOKENS, KV_HEADS, group, HD), jnp.float32)
    return values.reshape(TOKENS, HEADS * HD).astype(jnp.bfloat16)


def draw_kv_pool(key, part):
    key = jax.random.fold_in(key, 2)
    first = jax.random.fold_in(key, 0)
    values = jax.random.truncated_normal(first, -6.0, 6.0, (PAGES, PAGE, KV_HEADS, 2, HD), jnp.float32)
    return values.reshape(PAGES, PAGE, KV_HEADS * 2 * HD).astype(jnp.bfloat16)


def draw_fresh_kv(key, part):
    key = jax.random.fold_in(key, 3)
    first = jax.random.fold_in(key, 0)
    values = 2.5 * jax.random.truncated_normal(first, -6.0, 6.0, (TOKENS, KV_HEADS, 2, HD), jnp.float32)
    return values.reshape(TOKENS, KV_HEADS * 2 * HD).astype(jnp.bfloat16)


def draw_page_table(key, part):
    key = jax.random.fold_in(key, 4)
    ranks = N_DP
    shared_count = NODES_DEV // FAM * SHARED
    own_count = NODES_DEV * (PATH_PAGES - SHARED)
    keys = jax.random.split(key, 3)
    perm_shared = jax.vmap(lambda k: jax.random.permutation(k, shared_count))(jax.random.split(keys[0], ranks))
    perm_own = jax.vmap(lambda k: jax.random.permutation(k, own_count))(jax.random.split(keys[1], ranks))
    slots = jax.vmap(lambda k: jax.random.permutation(k, P_DEV))(jax.random.split(keys[2], ranks * ranks)).reshape(ranks, ranks, P_DEV)
    node = jnp.arange(NODES_DEV, dtype=jnp.int32)
    index_shared = (node // FAM)[:, None] * SHARED + jnp.arange(SHARED, dtype=jnp.int32)[None, :]
    index_own = node[:, None] * (PATH_PAGES - SHARED) + jnp.arange(PATH_PAGES - SHARED, dtype=jnp.int32)[None, :]

    def one_rank(shared_row, own_row, slot_rows):
        owner = jnp.concatenate([shared_row[index_shared] % ranks, own_row[index_own] % ranks], axis=1)
        place = jnp.concatenate([shared_row[index_shared] // ranks, shared_count // ranks + own_row[index_own] // ranks], axis=1)
        return owner * P_DEV + slot_rows[owner, place]
    table = jax.vmap(one_rank)(perm_shared, perm_own, slots)
    return table.reshape(ALL_NODES, PATH_PAGES).astype(jnp.int32)


def draw_path_len(key, part):
    key = jax.random.fold_in(key, 5)
    lengths = jax.random.randint(key, (ALL_NODES,), PATH - 4 * PAGE + 1, PATH + 1, jnp.int32)
    return jnp.where(jnp.arange(ALL_NODES) == 0, PATH, lengths).astype(jnp.int32)


def draw_parent(key, part):
    key = jax.random.fold_in(key, 6)
    first, second = jax.random.split(key)
    node = jnp.arange(ALL_NODES, dtype=jnp.int32)
    rank_pick = jax.random.randint(first, (ALL_NODES,), 0, N_DP, jnp.int32)
    slot_pick = jax.random.randint(second, (ALL_NODES,), 0, NODES_DEV // 2, jnp.int32)
    level_one = node % NODES_DEV < NODES_DEV // 2
    return jnp.where(level_one, -1, rank_pick * NODES_DEV + slot_pick).astype(jnp.int32)


def level_of(key, shape, cuts, least, high):
    def one(dim, parts):
        draws = jax.random.uniform(jax.random.fold_in(jax.random.fold_in(key, 6), dim), (parts,), jnp.float32, least / len(cuts), high / len(cuts))
        return jnp.repeat(jnp.exp(draws), shape[dim] // parts).reshape((-1,) + (1,) * (len(shape) - dim - 1))

    level = one(*cuts[0])
    for cut in cuts[1:]:
        level = level * one(*cut)
    return level


def bell_draw(stream_key, dims, spread, limit, cuts=(), kind=jnp.bfloat16):
    result = spread * jax.random.normal(stream_key, dims, jnp.float32)
    if cuts:
        result = result * level_of(stream_key, dims, cuts, -0.22, 0.18)
    return jnp.clip(result, -limit, limit).astype(kind)


def setup_inputs(seed: int = 0) -> dict:
    key_list = jax.random.split(jax.random.key(seed), 10)
    queries = draw_queries(jax.random.fold_in(key_list[9], 71), 0)
    fresh_kv = draw_fresh_kv(jax.random.fold_in(key_list[9], 71), 0)
    kv_pool = draw_kv_pool(jax.random.fold_in(key_list[9], 71), 0)
    page_table = draw_page_table(jax.random.fold_in(key_list[9], 71), 0)
    path_len = draw_path_len(jax.random.fold_in(key_list[9], 71), 0)
    parent = draw_parent(jax.random.fold_in(key_list[9], 71), 0)
    w_out = bell_draw(key_list[6], (HEADS * HD, D), 0.25, 4.0, ((0, 8),))
    residual = bell_draw(key_list[7], (TOKENS, D), 1.0, 6.0, ((0, 16),))
    gain = jnp.clip(1.0 + 0.1 * jax.random.normal(key_list[8], (D,), jnp.float32), 0.5, 1.5).astype(jnp.bfloat16)
    return dict(queries=queries, fresh_kv=fresh_kv, kv_pool=kv_pool, page_table=page_table, path_len=path_len, parent=parent, w_out=w_out, residual=residual, gain=gain)


def reference(queries, fresh_kv, kv_pool, page_table, path_len, parent, w_out, residual, gain):
    nodes_all = page_table.shape[0]
    group = HEADS // KV_HEADS
    span = PATH_PAGES * PAGE
    scale = HD ** (-0.5)
    q_all = queries.reshape(nodes_all, NEW, KV_HEADS, group, HD)
    fresh_all = fresh_kv.reshape(nodes_all, NEW, KV_HEADS, 2, HD)
    pool = kv_pool.reshape(kv_pool.shape[0], PAGE, KV_HEADS, 2, HD)

    def one_node(index):
        query = q_all[index].astype(jnp.float32)
        table = page_table[index]
        length = path_len[index]
        above = parent[index]
        path = jnp.take(pool, table, axis=0).reshape(span, KV_HEADS, 2, HD)
        own = fresh_all[index]
        upper = fresh_all[jnp.maximum(above, 0)]
        keys = jnp.concatenate([path, own, upper], axis=0).astype(jnp.float32)
        scores = jnp.einsum('tkgd,skd->ktgs', query, keys[:, :, 0]) * scale
        spot = jnp.arange(span + 2 * NEW)
        token = jnp.arange(NEW)
        in_path = (spot[None, :] < span) & (spot[None, :] < length)
        in_own = (spot[None, :] >= span) & (spot[None, :] < span + NEW) & (spot[None, :] - span <= token[:, None])
        in_upper = (spot[None, :] >= span + NEW) & (above >= 0)
        allowed = in_path | in_own | in_upper
        scores = jnp.where(allowed[None, :, None, :], scores, -jnp.inf)
        top = lax.optimization_barrier(jnp.max(scores, axis=-1, keepdims=True))
        weight = jnp.exp(scores - top)
        total = lax.optimization_barrier(jnp.sum(weight, axis=-1))
        rounded = lax.optimization_barrier(weight.astype(jnp.bfloat16)).astype(jnp.float32)
        out = jnp.einsum('ktgs,skd->ktgd', rounded, keys[:, :, 1]) / total[..., None]
        return out.transpose(1, 0, 2, 3).reshape(NEW, HEADS * HD)
    attn = lax.map(one_node, jnp.arange(nodes_all)).reshape(nodes_all * NEW, HEADS * HD).astype(jnp.bfloat16)
    cols = HEADS * HD // N_TENSOR
    summed = jnp.zeros((attn.shape[0], D), jnp.float32)
    for rank in range(N_TENSOR):
        part = jnp.dot(attn[:, rank * cols:(rank + 1) * cols], w_out[rank * cols:(rank + 1) * cols], preferred_element_type=jnp.float32)
        summed = summed + lax.optimization_barrier(part.astype(jnp.bfloat16)).astype(jnp.float32)
    mixed = residual.astype(jnp.float32) + summed
    power = lax.optimization_barrier(jnp.mean(mixed * mixed, axis=-1, keepdims=True))
    normed = mixed * lax.rsqrt(power + 1e-05) * gain.astype(jnp.float32)
    return (mixed.astype(jnp.bfloat16), normed.astype(jnp.bfloat16))
```

```python
import functools

import jax
import jax.numpy as jnp
from jax import lax
from jax.experimental import pallas as pl
from jax.experimental.pallas import tpu as pltpu
from jax.sharding import PartitionSpec as P

D = 8192
HD = 128
NEW = 16
PAGE = 64
PATH_PAGES = 16
SHARED = 8
FAM = 4
RANKS = 16
PAIR = 15
ROOTS = 12
LOG2E = 1.4426950408889634
MIB = 1024 * 1024


def pack_kernel(pages_dev, rank_ref, table_ref, pool_ref, send_ref, wanted_ref, wanted_smem, sem, sems):
    base = rank_ref[0] * pages_dev
    table = table_ref[...]
    lane = lax.broadcasted_iota(jnp.int32, (RANKS, 128), 1)
    present = jnp.zeros((RANKS, 128), jnp.float32)
    for page in range(pages_dev):
        hit = jnp.max((table == base + page).astype(jnp.float32), axis=1, keepdims=True)
        present = jnp.where(lane == page, hit, present)
    row = lax.broadcasted_iota(jnp.int32, (128, 128), 0)
    col = lax.broadcasted_iota(jnp.int32, (128, 128), 1)
    before = jnp.dot(
        present.astype(jnp.bfloat16),
        (row < col).astype(jnp.bfloat16),
        preferred_element_type=jnp.float32,
    )
    place = jnp.where(present > 0, before, -1.0)
    wanted = jnp.zeros((RANKS, 128), jnp.float32)
    lane_f = lane.astype(jnp.float32)
    for slot in range(PAIR):
        page = jnp.sum(jnp.where(place == slot, lane_f, 0.0), axis=1, keepdims=True)
        wanted = jnp.where(lane == slot, page, wanted)
    wanted_ref[...] = wanted.astype(jnp.int32)
    copy = pltpu.make_async_copy(wanted_ref, wanted_smem, sem)
    copy.start()
    copy.wait()

    @pl.loop(0, RANKS)
    def _(dest):
        for slot in range(PAIR):
            page = jnp.clip(wanted_smem[dest, slot], 0, pages_dev - 1)
            pltpu.make_async_copy(pool_ref.at[page], send_ref.at[dest, slot], sems).start()

    pltpu.make_async_copy(send_ref, send_ref, sems).wait()


def pack(rank, table, pool):
    pages_dev = pool.shape[0]
    return pl.pallas_call(
        functools.partial(pack_kernel, pages_dev),
        out_shape=jax.ShapeDtypeStruct((RANKS, PAIR) + pool.shape[1:], pool.dtype),
        in_specs=[
            pl.BlockSpec(memory_space=pltpu.SMEM),
            pl.BlockSpec(memory_space=pltpu.VMEM),
            pl.BlockSpec(memory_space=pltpu.VMEM),
        ],
        out_specs=pl.BlockSpec(memory_space=pl.ANY),
        scratch_shapes=[
            pltpu.VMEM((RANKS, 128), jnp.int32),
            pltpu.SMEM((RANKS, 128), jnp.int32),
            pltpu.SemaphoreType.DMA,
            pltpu.SemaphoreType.DMA,
        ],
        name="pack_pages",
    )(rank, table, pool)


def attend_kernel(idx_ref, len_ref, parent_ref, q_ref, fresh_ref, roots_ref, recv_ref, out_ref):
    family = pl.program_id(0)
    scale = HD ** (-0.5) * LOG2E
    nt = (((1,), (1,)), ((), ()))

    def pages(node, first):
        blocks = [recv_ref[idx_ref[node * PATH_PAGES + first + s]] for s in range(SHARED)]
        return jnp.concatenate(blocks, axis=0)

    shared = pages(family * FAM, 0)
    q_nodes = []
    for i in range(FAM):
        rows = q_ref[i * NEW : (i + 1) * NEW, :]
        heads = rows.shape[1] // HD
        q_nodes.append(jnp.concatenate([rows[:, h * HD : (h + 1) * HD] for h in range(heads)], axis=0))
    query = jnp.concatenate(q_nodes, axis=0)
    span = q_nodes[0].shape[0]
    s_shared = lax.dot_general(query, shared[:, :HD], nt, preferred_element_type=jnp.float32)
    top_shared = jnp.max(s_shared, axis=1, keepdims=True)
    tops, totals, accums = [], [], []
    for i in range(FAM):
        node = family * FAM + i
        above = parent_ref[node]
        own = pages(node, SHARED)
        start = pl.multiple_of(jnp.maximum(above, 0) * NEW, NEW)
        near = jnp.concatenate(
            [fresh_ref[i * NEW : (i + 1) * NEW, :], roots_ref[pl.ds(start, NEW), :]], axis=0
        )
        s_own = lax.dot_general(q_nodes[i], own[:, :HD], nt, preferred_element_type=jnp.float32)
        s_near = lax.dot_general(q_nodes[i], near[:, :HD], nt, preferred_element_type=jnp.float32)
        spot = lax.broadcasted_iota(jnp.int32, s_own.shape, 1) + SHARED * PAGE
        s_own = jnp.where(spot < len_ref[node], s_own, -jnp.inf)
        token = lax.broadcasted_iota(jnp.int32, s_near.shape, 0) % NEW
        key = lax.broadcasted_iota(jnp.int32, s_near.shape, 1)
        allowed = (key <= token) | ((key >= NEW) & (above >= 0))
        s_near = jnp.where(allowed, s_near, -jnp.inf)
        top = jnp.maximum(
            jnp.maximum(top_shared[i * span : (i + 1) * span], jnp.max(s_own, axis=1, keepdims=True)),
            jnp.max(s_near, axis=1, keepdims=True),
        )
        w_own = jnp.exp2((s_own - top) * scale)
        w_near = jnp.exp2((s_near - top) * scale)
        totals.append(jnp.sum(w_own, axis=1, keepdims=True) + jnp.sum(w_near, axis=1, keepdims=True))
        accums.append(
            jnp.dot(w_own.astype(jnp.bfloat16), own[:, HD:], preferred_element_type=jnp.float32)
            + jnp.dot(w_near.astype(jnp.bfloat16), near[:, HD:], preferred_element_type=jnp.float32)
        )
        tops.append(top)
    top = jnp.concatenate(tops, axis=0)
    w_shared = jnp.exp2((s_shared - top) * scale)
    total = jnp.concatenate(totals, axis=0) + jnp.sum(w_shared, axis=1, keepdims=True)
    accum = jnp.concatenate(accums, axis=0) + jnp.dot(
        w_shared.astype(jnp.bfloat16), shared[:, HD:], preferred_element_type=jnp.float32
    )
    attn = (accum / total).astype(jnp.bfloat16)
    for i in range(FAM):
        for h in range(span // NEW):
            block = attn[i * span + h * NEW : i * span + (h + 1) * NEW, :]
            out_ref[i * NEW : (i + 1) * NEW, h * HD : (h + 1) * HD] = block


def attend(idx, lengths, above, queries, fresh, roots, received):
    rows, width = queries.shape
    step = FAM * NEW
    pages = received.shape[0]
    return pl.pallas_call(
        attend_kernel,
        out_shape=jax.ShapeDtypeStruct((rows, width), jnp.bfloat16),
        grid_spec=pltpu.PrefetchScalarGridSpec(
            num_scalar_prefetch=3,
            grid=(rows // step,),
            in_specs=[
                pl.BlockSpec((step, width), lambda f, *_: (f, 0)),
                pl.BlockSpec((step, fresh.shape[1]), lambda f, *_: (f, 0)),
                pl.BlockSpec(memory_space=pltpu.VMEM),
                pl.BlockSpec(memory_space=pltpu.VMEM),
            ],
            out_specs=pl.BlockSpec((step, width), lambda f, *_: (f, 0)),
        ),
        compiler_params=pltpu.CompilerParams(vmem_limit_bytes=40 * MIB),
        cost_estimate=pl.CostEstimate(
            flops=4 * rows * width * 1056, bytes_accessed=pages * PAGE * 512 + 4 * rows * width, transcendentals=rows * 8 * 1056
        ),
        name="attend",
    )(idx, lengths, above, queries, fresh, roots, received)


def project_kernel(attn_ref, w_ref, out_ref):
    out_ref[0] = jnp.dot(attn_ref[...], w_ref[...], preferred_element_type=jnp.float32).astype(jnp.bfloat16)


def project(attn, w_out, parts):
    rows, depth = attn.shape
    cols = w_out.shape[1] // parts
    half = cols // 2
    return pl.pallas_call(
        project_kernel,
        out_shape=jax.ShapeDtypeStruct((parts, rows, cols), jnp.bfloat16),
        grid=(parts, 2),
        in_specs=[
            pl.BlockSpec((rows, depth), lambda p, c: (0, 0)),
            pl.BlockSpec((depth, half), lambda p, c: (0, p * 2 + c)),
        ],
        out_specs=pl.BlockSpec((1, rows, half), lambda p, c: (p, 0, c)),
        compiler_params=pltpu.CompilerParams(vmem_limit_bytes=40 * MIB),
        cost_estimate=pl.CostEstimate(
            flops=2 * rows * depth * w_out.shape[1], bytes_accessed=w_out.size * 2 + rows * w_out.shape[1] * 2, transcendentals=0
        ),
        name="project",
    )(attn, w_out)


def share_roots(fresh):
    def along(dy, dx):
        return [(s, (s // 4 + dy) % 4 * 4 + (s % 4 + dx) % 4) for s in range(RANKS)]

    mine = fresh[: ROOTS * NEW]
    row = jnp.concatenate([mine] + [lax.ppermute(mine, "dp", along(0, d)) for d in (1, 2, 3)], axis=0)
    return jnp.concatenate([row] + [lax.ppermute(row, "dp", along(d, 0)) for d in (1, 2, 3)], axis=0)


def slots_of(table, ranks, pages_dev):
    owner = table // pages_dev
    page = jnp.arange(ranks * pages_dev, dtype=jnp.int32)
    present = jnp.any(table[None, :] == page[:, None], axis=1)
    place = jnp.sum(
        (present[None, :] & (page[None, :] // pages_dev == owner[:, None]) & (page[None, :] < table[:, None])).astype(jnp.int32),
        axis=1,
    )
    return owner * PAIR + place


def body(queries, fresh_kv, kv_pool, page_table, path_len, parent, w_out, residual, gain):
    rank = lax.axis_index("dp")
    tensor_rank = lax.axis_index("tensor")
    tensors = lax.axis_size("tensor")
    rows = queries.shape[0]
    nodes = rows // NEW
    pages_dev = kv_pool.shape[0]
    dest_table = page_table.reshape(RANKS, nodes * PATH_PAGES)
    send = pack(rank.reshape(1), dest_table, kv_pool)
    received = lax.all_to_all(send, "dp", split_axis=0, concat_axis=0, tiled=True)
    received = received.reshape(RANKS * PAIR, PAGE, kv_pool.shape[2])
    roots = share_roots(fresh_kv)

    own_table = lax.dynamic_index_in_dim(dest_table, rank, 0, keepdims=False)
    idx = slots_of(own_table, RANKS, pages_dev)
    lengths = lax.dynamic_slice_in_dim(path_len, rank * nodes, nodes)
    above = lax.dynamic_slice_in_dim(parent, rank * nodes, nodes)
    up_rank, up_node = above // nodes, above % nodes
    away_y = (rank // 4 - up_rank // 4) % 4
    away_x = (rank % 4 - up_rank % 4) % 4
    above = jnp.where(above >= 0, (away_y * 4 + away_x) * ROOTS + up_node, -1)

    attn = attend(idx, lengths, above, queries, fresh_kv, roots, received)
    parts = project(attn, w_out, tensors)
    summed = lax.psum_scatter(parts, "tensor", scatter_dimension=0, tiled=True)[0]
    cols = summed.shape[1]
    kept = lax.dynamic_slice_in_dim(residual, tensor_rank * cols, cols, 1)
    mixed = kept.astype(jnp.float32) + summed.astype(jnp.float32)
    power = jnp.sum(mixed * mixed, axis=1).reshape(rows // 128, 128)
    total = power
    for d in range(1, tensors):
        total = total + lax.ppermute(power, "tensor", [(t, (t + d) % tensors) for t in range(tensors)])
    norm = lax.rsqrt(total.reshape(rows, 1) / D + 1e-05)
    own_gain = lax.dynamic_slice_in_dim(gain, tensor_rank * cols, cols)
    normed = mixed * norm * own_gain.astype(jnp.float32)
    return (mixed.astype(jnp.bfloat16), normed.astype(jnp.bfloat16))


def solution(mesh):
    return jax.shard_map(
        body,
        mesh=mesh,
        in_specs=(
            P("dp", "tensor"),
            P("dp", "tensor"),
            P("dp", None, "tensor"),
            P(),
            P(),
            P(),
            P("tensor", None),
            P("dp", None),
            P(),
        ),
        out_specs=(P("dp", "tensor"), P("dp", "tensor")),
        check_vma=False,
    )
```

```python
import functools

import jax
import jax.numpy as jnp
from jax import lax
from jax.experimental import pallas as pl
from jax.experimental.pallas import tpu as pltpu
from jax.sharding import PartitionSpec as P

D = 8192
HD = 128
NEW = 16
PAGE = 64
PATH_PAGES = 16
SHARED = 8
FAM = 4
RANKS = 16
PAIR = 15
ROOTS = 12
FIRST = 3
LOG2E = 1.4426950408889634
MIB = 1024 * 1024


def pack_kernel(rank_ref, table_ref, pool_ref, send_ref, wanted_ref, wanted_smem, sem, send_sem):
    pages_dev = pool_ref.shape[0]
    slots, nodes = table_ref.shape
    base = rank_ref[0] * pages_dev
    table = table_ref[...]
    height = -(-pages_dev // 16) * 16
    row = lax.broadcasted_iota(jnp.int32, (height, nodes), 0)
    hits = jnp.zeros((height, nodes), jnp.float32)
    for page in range(pages_dev):
        hit = jnp.max((table == base + page).astype(jnp.float32), axis=0, keepdims=True)
        hits = jnp.where(row == page, hit, hits)
    node = lax.broadcasted_iota(jnp.int32, (nodes, 128), 0)
    begin = lax.broadcasted_iota(jnp.int32, (nodes, 128), 1) * (nodes // RANKS)
    belongs = ((node >= begin) & (node < begin + nodes // RANKS)).astype(jnp.bfloat16)
    present = jnp.dot(hits.astype(jnp.bfloat16), belongs, preferred_element_type=jnp.float32) > 0
    low = lax.broadcasted_iota(jnp.int32, (height, height), 0)
    high = lax.broadcasted_iota(jnp.int32, (height, height), 1)
    before = jnp.dot(
        (high < low).astype(jnp.bfloat16), present.astype(jnp.bfloat16), preferred_element_type=jnp.float32
    )
    place = jnp.where(present, before, -1.0)
    page_id = lax.broadcasted_iota(jnp.int32, (height, 128), 0).astype(jnp.float32)
    line = lax.broadcasted_iota(jnp.int32, (16, 128), 0)
    wanted = jnp.zeros((16, 128), jnp.float32)
    for slot in range(PAIR):
        page = jnp.sum(jnp.where(place == slot, page_id, 0.0), axis=0, keepdims=True)
        wanted = jnp.where(line == slot, page, wanted)
    wanted_ref[...] = wanted.astype(jnp.int32)
    copy = pltpu.make_async_copy(wanted_ref, wanted_smem, sem)
    copy.start()
    copy.wait()

    @pl.loop(0, RANKS)
    def _(dest):
        for slot in range(PAIR):
            page = jnp.clip(wanted_smem[slot, dest], 0, pages_dev - 1)
            pltpu.make_async_copy(pool_ref.at[page], send_ref.at[dest, slot], send_sem).start()

    pltpu.make_async_copy(send_ref, send_ref, send_sem).wait()


def pack(rank, table, pool):
    return pl.pallas_call(
        pack_kernel,
        out_shape=jax.ShapeDtypeStruct((RANKS, PAIR) + pool.shape[1:], pool.dtype),
        in_specs=[
            pl.BlockSpec(memory_space=pltpu.SMEM),
            pl.BlockSpec(memory_space=pltpu.VMEM),
            pl.BlockSpec(memory_space=pltpu.VMEM),
        ],
        out_specs=pl.BlockSpec(memory_space=pltpu.HBM),
        scratch_shapes=[
            pltpu.VMEM((16, 128), jnp.int32),
            pltpu.SMEM((16, 128), jnp.int32),
            pltpu.SemaphoreType.DMA,
            pltpu.SemaphoreType.DMA,
        ],
        name="pack_pages",
    )(rank, table, pool)


def attend_family(first, node, idx_ref, len_ref, above_ref, q_ref, fresh_ref, roots_ref, pages_ref, attn_ref):
    scale = HD ** (-0.5) * LOG2E
    nt = (((1,), (1,)), ((), ()))

    def pages(n, slot):
        return jnp.concatenate([pages_ref[idx_ref[n * PATH_PAGES + slot + s]] for s in range(SHARED)], axis=0)

    heads = q_ref.shape[1] // HD
    span = heads * NEW
    shared = pages(node, 0)
    queries = []
    for i in range(FAM):
        rows = q_ref[first + i * NEW : first + (i + 1) * NEW, :]
        queries.append(jnp.concatenate([rows[:, h * HD : (h + 1) * HD] for h in range(heads)], axis=0))
    s_shared = lax.dot_general(
        jnp.concatenate(queries, axis=0), shared[:, :HD], nt, preferred_element_type=jnp.float32
    )
    half = SHARED * PAGE // 2
    own, s_own = [], []
    for i in range(FAM):
        above = above_ref[node + i]
        start = pl.multiple_of(jnp.maximum(above, 0) * NEW, NEW)
        fresh = fresh_ref[first + i * NEW : first + (i + 1) * NEW, :]
        kv = jnp.concatenate([pages(node + i, SHARED), fresh, roots_ref[pl.ds(start, NEW), :]], axis=0)
        s = lax.dot_general(queries[i], kv[:, :HD], nt, preferred_element_type=jnp.float32)
        late = s[:, half:]
        spot = lax.broadcasted_iota(jnp.int32, late.shape, 1) + SHARED * PAGE + half
        token = lax.broadcasted_iota(jnp.int32, late.shape, 0) % NEW
        key = spot - PATH_PAGES * PAGE
        limit = jnp.where(above >= 0, 2 * NEW, NEW)
        allowed = (spot < len_ref[node + i]) | ((key >= 0) & (key <= token)) | ((key >= NEW) & (key < limit))
        own.append(kv)
        s_own.append(jnp.concatenate([s[:, :half], jnp.where(allowed, late, -jnp.inf)], axis=1))
    tops = [
        jnp.maximum(
            jnp.max(s_shared[i * span : (i + 1) * span], axis=1, keepdims=True),
            jnp.max(s_own[i], axis=1, keepdims=True),
        )
        for i in range(FAM)
    ]
    w_own = [jnp.exp2((s_own[i] - tops[i]) * scale).astype(jnp.bfloat16) for i in range(FAM)]
    w_shared = jnp.exp2((s_shared - jnp.concatenate(tops, axis=0)) * scale).astype(jnp.bfloat16)
    ones = jnp.ones((own[0].shape[0], HD), jnp.bfloat16)
    accum = [
        jnp.dot(w_own[i], jnp.concatenate([own[i][:, HD:], ones], axis=1), preferred_element_type=jnp.float32)
        for i in range(FAM)
    ]
    accum = jnp.concatenate(accum, axis=0) + jnp.dot(
        w_shared, jnp.concatenate([shared[:, HD:], ones[: SHARED * PAGE]], axis=1), preferred_element_type=jnp.float32
    )
    attn = (accum[:, :HD] / accum[:, HD:]).astype(jnp.bfloat16)
    for i in range(FAM):
        for h in range(heads):
            block = attn[i * span + h * NEW : i * span + (h + 1) * NEW, :]
            attn_ref[first + i * NEW : first + (i + 1) * NEW, h * HD : (h + 1) * HD] = block


def rollout_kernel(
    node0, families, counts, idx_ref, len_ref, above_ref, order_ref, q_ref, fresh_ref, roots_ref, pages_ref, w_ref, *refs
):
    outs, (attn_ref, stage, out_sem) = refs[: len(counts)], refs[len(counts) :]
    blocks, _, cols = stage.shape
    for f in range(families):
        attend_family(
            f * FAM * NEW, node0 + f * FAM, idx_ref, len_ref, above_ref, q_ref, fresh_ref, roots_ref, pages_ref, attn_ref
        )
    base = 0
    for out, count in zip(outs, counts):

        @pl.loop(0, count)
        def _(b):
            slot = base + b
            start = pl.multiple_of(order_ref[slot] * cols, cols)
            w = w_ref[:, pl.ds(start, cols)]
            stage[slot] = jnp.dot(attn_ref[...], w, preferred_element_type=jnp.float32).astype(jnp.bfloat16)
            pltpu.make_async_copy(stage.at[slot], out.at[b], out_sem).start()

        base += count
    base = 0
    for out, count in zip(outs, counts):
        pltpu.make_async_copy(stage.at[pl.ds(base, count)], out, out_sem).wait()
        base += count


def rollout(node0, families, counts, idx, lengths, above, order, queries, fresh, roots, received, w_out):
    width = queries.shape[1]
    rows = families * FAM * NEW
    first = node0 * NEW
    blocks = sum(counts)
    cols = w_out.shape[1] // blocks
    smem = pl.BlockSpec(memory_space=pltpu.SMEM)
    vmem = pl.BlockSpec(memory_space=pltpu.VMEM)
    hbm = pl.BlockSpec(memory_space=pltpu.HBM)
    return pl.pallas_call(
        functools.partial(rollout_kernel, node0, families, counts),
        out_shape=[jax.ShapeDtypeStruct((count, rows, cols), jnp.bfloat16) for count in counts],
        in_specs=[smem, smem, smem, smem, vmem, vmem, vmem, vmem, vmem],
        out_specs=[hbm] * len(counts),
        scratch_shapes=[
            pltpu.VMEM((rows, width), jnp.bfloat16),
            pltpu.VMEM((blocks, rows, cols), jnp.bfloat16),
            pltpu.SemaphoreType.DMA,
        ],
        compiler_params=pltpu.CompilerParams(vmem_limit_bytes=24 * MIB),
        cost_estimate=pl.CostEstimate(
            flops=4 * rows * width * 1056 + 2 * rows * width * w_out.shape[1],
            bytes_accessed=received.size * 2 + w_out.size * 2 + rows * w_out.shape[1] * 2,
            transcendentals=rows * 8 * 1056,
        ),
        name="rollout",
    )(idx, lengths, above, order, queries[first : first + rows], fresh[first : first + rows], roots, received, w_out)


def shift(dy, dx):
    return [(s, (s // 4 + dy) % 4 * 4 + (s % 4 + dx) % 4) for s in range(RANKS)]


def turn(d):
    return [(t, (t + 2 * d) % 8) for t in range(8)]


def gather_row(fresh):
    mine = fresh[: ROOTS * NEW]
    return jnp.concatenate([mine] + [lax.ppermute(mine, "dp", shift(0, d)) for d in (1, 2, 3)], axis=0)


def deliver_parents(row, rank, parent, nodes):
    y, x = rank // 4, rank % 4
    column = lax.dynamic_index_in_dim(parent.reshape(4, 4, nodes), x, 1, keepdims=False)
    column = lax.dynamic_slice_in_dim(jnp.concatenate([column, column], axis=0), y, 4)
    named = jnp.maximum(column[:, ROOTS:], 0)
    away = (x - named // nodes % 4) % 4
    places = jnp.clip(away * ROOTS + named % nodes, 0, 4 * ROOTS - 1).reshape(-1)
    picked = jnp.take(row.reshape(4 * ROOTS, NEW, row.shape[1]), places, axis=0, mode="clip")
    picked = picked.reshape(4, (nodes - ROOTS) * NEW, row.shape[1])
    got = [picked[0]] + [lax.ppermute(picked[d], "dp", shift(d, 0)) for d in (1, 2, 3)]
    own = column[0]
    child = jnp.arange(nodes, dtype=jnp.int32) - ROOTS
    up = (y - jnp.maximum(own, 0) // nodes // 4) % 4 * (nodes - ROOTS) + child
    return jnp.concatenate(got, axis=0), jnp.where((own >= 0) & (child >= 0), up, -1)


def slots_of(table, ranks, pages_dev):
    owner = table // pages_dev
    page = jnp.arange(ranks * pages_dev, dtype=jnp.int32)
    present = jnp.any(table[None, :] == page[:, None], axis=1)
    place = jnp.sum(
        (present[None, :] & (page[None, :] // pages_dev == owner[:, None]) & (page[None, :] < table[:, None])).astype(jnp.int32),
        axis=1,
    )
    return owner * PAIR + place


def body(queries, fresh_kv, kv_pool, page_table, path_len, parent, w_out, residual, gain):
    rank = lax.axis_index("dp")
    tensor_rank = lax.axis_index("tensor")
    tensors = lax.axis_size("tensor")
    rows = queries.shape[0]
    nodes = rows // NEW
    pages_dev = kv_pool.shape[0]
    row = gather_row(fresh_kv)
    send = pack(rank.reshape(1), page_table.T, kv_pool)
    send, row, page_table, path_len, parent = lax.optimization_barrier((send, row, page_table, path_len, parent))
    received = lax.all_to_all(send, "dp", split_axis=0, concat_axis=0, tiled=True)
    received = received.reshape(RANKS * PAIR, PAGE, kv_pool.shape[2])
    roots, above = deliver_parents(row, rank, parent, nodes)

    own_table = lax.dynamic_slice_in_dim(page_table, rank * nodes, nodes).reshape(-1)
    idx = slots_of(own_table, RANKS, pages_dev)
    lengths = lax.dynamic_slice_in_dim(path_len, rank * nodes, nodes)

    z, core = tensor_rank // 2, tensor_rank % 2
    around = (z + jnp.arange(4, dtype=jnp.int32)) % 4 * 2
    order = jnp.concatenate([around + 1 - core, around + core])
    plain = jnp.arange(tensors, dtype=jnp.int32)
    args = (queries, fresh_kv, roots, received, w_out)
    early = FIRST * FAM
    (parts,) = rollout(0, FIRST, (tensors,), idx, lengths, above, plain, *args)
    parts, order = lax.optimization_barrier((parts, order))
    summed_a = lax.psum_scatter(parts, "tensor", scatter_dimension=0, tiled=True)[0].astype(jnp.float32)

    away, kept = rollout(early, nodes // FAM - FIRST, (4, 4), idx, lengths, above, order, *args)
    back = lax.ppermute(away, "tensor", [(t, t ^ 1) for t in range(tensors)])

    def pair(i):
        return kept[i].astype(jnp.float32) + back[i].astype(jnp.float32)

    half = kept.shape[1] // 2
    far = pair(2).astype(jnp.bfloat16)
    from_low = lax.ppermute(far[:half], "tensor", turn(1)).astype(jnp.float32)
    from_high = lax.ppermute(far[half:], "tensor", turn(-1)).astype(jnp.float32)
    up, down = pair(1), pair(3)
    up = jnp.concatenate([up[:half] + from_low, up[half:]], axis=0).astype(jnp.bfloat16)
    down = jnp.concatenate([down[:half], down[half:] + from_high], axis=0).astype(jnp.bfloat16)
    summed_b = (
        pair(0)
        + lax.ppermute(up, "tensor", turn(1)).astype(jnp.float32)
        + lax.ppermute(down, "tensor", turn(-1)).astype(jnp.float32)
    )

    cols = summed_a.shape[1]
    mine = lax.dynamic_slice_in_dim(residual, tensor_rank * cols, cols, 1)
    mixed = mine.astype(jnp.float32) + jnp.concatenate([summed_a, summed_b], axis=0)
    power = jnp.sum(mixed * mixed, axis=1).reshape(rows // 128, 128)
    power = power + lax.ppermute(power, "tensor", [(t, t ^ 1) for t in range(tensors)])
    total = power
    for d in (1, 2, 3):
        total = total + lax.ppermute(power, "tensor", turn(d))
    norm = lax.rsqrt(total.reshape(rows, 1) / D + 1e-05)
    own_gain = lax.dynamic_slice_in_dim(gain, tensor_rank * cols, cols)
    normed = mixed * norm * own_gain.astype(jnp.float32)
    return (mixed.astype(jnp.bfloat16), normed.astype(jnp.bfloat16))


def solution(mesh):
    return jax.shard_map(
        body,
        mesh=mesh,
        in_specs=(
            P("dp", "tensor"),
            P("dp", "tensor"),
            P("dp", None, "tensor"),
            P(),
            P(),
            P(),
            P("tensor", None),
            P("dp", None),
            P(),
        ),
        out_specs=(P("dp", "tensor"), P("dp", "tensor")),
        check_vma=False,
    )
```

```python
import functools

import jax
import jax.numpy as jnp
from jax import lax
from jax.experimental import pallas as pl
from jax.experimental.pallas import tpu as pltpu
from jax.sharding import PartitionSpec as P

D = 8192
HD = 128
NEW = 16
PAGE = 64
PATH_PAGES = 16
SHARED = 8
FAM = 4
RANKS = 16
PAIR = 15
ROOTS = 12
SHARE = 3
GROUPS = (3, 3)
LOG2E = 1.4426950408889634
MIB = 1024 * 1024


def pack_kernel(rank_ref, table_ref, pool_ref, send_ref, wanted_ref, wanted_smem, sem, send_sem):
    pages_dev = pool_ref.shape[0]
    slots, nodes = table_ref.shape
    base = rank_ref[0] * pages_dev
    table = table_ref[...]
    height = -(-pages_dev // 16) * 16
    row = lax.broadcasted_iota(jnp.int32, (height, nodes), 0)
    hits = jnp.zeros((height, nodes), jnp.float32)
    for page in range(pages_dev):
        hit = jnp.max((table == base + page).astype(jnp.float32), axis=0, keepdims=True)
        hits = jnp.where(row == page, hit, hits)
    node = lax.broadcasted_iota(jnp.int32, (nodes, 128), 0)
    begin = lax.broadcasted_iota(jnp.int32, (nodes, 128), 1) * (nodes // RANKS)
    belongs = ((node >= begin) & (node < begin + nodes // RANKS)).astype(jnp.bfloat16)
    present = jnp.dot(hits.astype(jnp.bfloat16), belongs, preferred_element_type=jnp.float32) > 0
    low = lax.broadcasted_iota(jnp.int32, (height, height), 0)
    high = lax.broadcasted_iota(jnp.int32, (height, height), 1)
    before = jnp.dot(
        (high < low).astype(jnp.bfloat16), present.astype(jnp.bfloat16), preferred_element_type=jnp.float32
    )
    place = jnp.where(present, before, -1.0)
    page_id = lax.broadcasted_iota(jnp.int32, (height, 128), 0).astype(jnp.float32)
    line = lax.broadcasted_iota(jnp.int32, (16, 128), 0)
    wanted = jnp.zeros((16, 128), jnp.float32)
    for slot in range(PAIR):
        page = jnp.sum(jnp.where(place == slot, page_id, 0.0), axis=0, keepdims=True)
        wanted = jnp.where(line == slot, page, wanted)
    wanted_ref[...] = wanted.astype(jnp.int32)
    copy = pltpu.make_async_copy(wanted_ref, wanted_smem, sem)
    copy.start()
    copy.wait()

    @pl.loop(0, RANKS)
    def _(dest):
        for slot in range(PAIR):
            page = jnp.clip(wanted_smem[slot, dest], 0, pages_dev - 1)
            pltpu.make_async_copy(pool_ref.at[page], send_ref.at[dest, slot], send_sem).start()

    filled = send_ref.at[:, pl.ds(0, PAIR)]
    pltpu.make_async_copy(filled, filled, send_sem).wait()


def pack(rank, table, pool):
    return pl.pallas_call(
        pack_kernel,
        out_shape=jax.ShapeDtypeStruct((RANKS, PAIR + 1) + pool.shape[1:], pool.dtype),
        in_specs=[
            pl.BlockSpec(memory_space=pltpu.SMEM),
            pl.BlockSpec(memory_space=pltpu.VMEM),
            pl.BlockSpec(memory_space=pltpu.VMEM),
        ],
        out_specs=pl.BlockSpec(memory_space=pltpu.HBM),
        scratch_shapes=[
            pltpu.VMEM((16, 128), jnp.int32),
            pltpu.SMEM((16, 128), jnp.int32),
            pltpu.SemaphoreType.DMA,
            pltpu.SemaphoreType.DMA,
        ],
        name="pack_pages",
    )(rank, table, pool)


def pack_parents_kernel(rank_ref, parent_ref, row_ref, _, send_ref, sem):
    y, x = rank_ref[0] // 4, rank_ref[0] % 4
    nodes = parent_ref.shape[0] // RANKS

    def copy(dest, i, place):
        source = row_ref.at[pl.ds(pl.multiple_of(place * NEW, NEW), NEW)]
        return pltpu.make_async_copy(source, send_ref.at[dest, PAIR, pl.ds(i * NEW, NEW)], sem)

    @pl.loop(0, RANKS)
    def _(dest):
        for i in range(SHARE):
            named = jnp.maximum(parent_ref[dest * nodes + ROOTS + x * SHARE + i], 0)
            away = (x + 4 - named // nodes % 4) % 4
            copy(dest, i, jnp.minimum(away * ROOTS + named % nodes, 4 * ROOTS - 1)).start()

    filled = send_ref.at[:, PAIR, pl.ds(0, SHARE * NEW)]
    pltpu.make_async_copy(filled, filled, sem).wait()


def pack_parents(rank, parent, row, send):
    smem = pl.BlockSpec(memory_space=pltpu.SMEM)
    hbm = pl.BlockSpec(memory_space=pltpu.HBM)
    return pl.pallas_call(
        pack_parents_kernel,
        out_shape=jax.ShapeDtypeStruct(send.shape, send.dtype),
        in_specs=[smem, smem, pl.BlockSpec(memory_space=pltpu.VMEM), hbm],
        out_specs=hbm,
        scratch_shapes=[pltpu.SemaphoreType.DMA],
        input_output_aliases={3: 0},
        name="pack_parents",
    )(rank, parent, row, send)


def attend_family(first, node, idx_ref, len_ref, above_ref, q_ref, fresh_ref, pages_ref, attn_ref):
    scale = HD ** (-0.5) * LOG2E
    nt = (((1,), (1,)), ((), ()))

    def pages(n, slot):
        return jnp.concatenate([pages_ref[idx_ref[n * PATH_PAGES + slot + s]] for s in range(SHARED)], axis=0)

    heads = q_ref.shape[1] // HD
    span = heads * NEW
    shared = pages(node, 0)
    queries = []
    for i in range(FAM):
        rows = q_ref[first + i * NEW : first + (i + 1) * NEW, :]
        queries.append(jnp.concatenate([rows[:, h * HD : (h + 1) * HD] for h in range(heads)], axis=0))
    s_shared = lax.dot_general(
        jnp.concatenate(queries, axis=0), shared[:, :HD], nt, preferred_element_type=jnp.float32
    )
    half = SHARED * PAGE // 2
    own, s_own = [], []
    for i in range(FAM):
        above = above_ref[node + i]
        spot = jnp.maximum(above, 0)
        upper = pages_ref[spot // PAGE, pl.ds(pl.multiple_of(spot % PAGE, NEW), NEW), :]
        fresh = fresh_ref[first + i * NEW : first + (i + 1) * NEW, :]
        kv = jnp.concatenate([pages(node + i, SHARED), fresh, upper], axis=0)
        s = lax.dot_general(queries[i], kv[:, :HD], nt, preferred_element_type=jnp.float32)
        late = s[:, half:]
        spot = lax.broadcasted_iota(jnp.int32, late.shape, 1) + SHARED * PAGE + half
        token = lax.broadcasted_iota(jnp.int32, late.shape, 0) % NEW
        key = spot - PATH_PAGES * PAGE
        limit = jnp.where(above >= 0, 2 * NEW, NEW)
        allowed = (spot < len_ref[node + i]) | ((key >= 0) & (key <= token)) | ((key >= NEW) & (key < limit))
        own.append(kv)
        s_own.append(jnp.concatenate([s[:, :half], jnp.where(allowed, late, -jnp.inf)], axis=1))
    tops = [
        jnp.maximum(
            jnp.max(s_shared[i * span : (i + 1) * span], axis=1, keepdims=True),
            jnp.max(s_own[i], axis=1, keepdims=True),
        )
        for i in range(FAM)
    ]
    w_own = [jnp.exp2((s_own[i] - tops[i]) * scale).astype(jnp.bfloat16) for i in range(FAM)]
    w_shared = jnp.exp2((s_shared - jnp.concatenate(tops, axis=0)) * scale).astype(jnp.bfloat16)
    ones = jnp.ones((own[0].shape[0], HD), jnp.bfloat16)
    accum = [
        jnp.dot(w_own[i], jnp.concatenate([own[i][:, HD:], ones], axis=1), preferred_element_type=jnp.float32)
        for i in range(FAM)
    ]
    accum = jnp.concatenate(accum, axis=0) + jnp.dot(
        w_shared, jnp.concatenate([shared[:, HD:], ones[: SHARED * PAGE]], axis=1), preferred_element_type=jnp.float32
    )
    attn = (accum[:, :HD] / accum[:, HD:]).astype(jnp.bfloat16)
    for i in range(FAM):
        for h in range(heads):
            block = attn[i * span + h * NEW : i * span + (h + 1) * NEW, :]
            attn_ref[first + i * NEW : first + (i + 1) * NEW, h * HD : (h + 1) * HD] = block


def attend_kernel(idx_ref, len_ref, above_ref, q_ref, fresh_ref, recv_ref, attn_ref, pages_ref, sem):
    ranks = RANKS * (PAIR + 1)
    for r in range(RANKS):
        part = pl.ds(r * (ranks // RANKS), ranks // RANKS)
        pltpu.make_async_copy(recv_ref.at[part], pages_ref.at[part], sem).start()
    pltpu.make_async_copy(recv_ref, pages_ref, sem).wait()
    for f in range(q_ref.shape[0] // (FAM * NEW)):
        attend_family(f * FAM * NEW, f * FAM, idx_ref, len_ref, above_ref, q_ref, fresh_ref, pages_ref, attn_ref)


def attend(idx, lengths, above, queries, fresh, received):
    rows, width = queries.shape
    smem = pl.BlockSpec(memory_space=pltpu.SMEM)
    vmem = pl.BlockSpec(memory_space=pltpu.VMEM)
    return pl.pallas_call(
        attend_kernel,
        out_shape=jax.ShapeDtypeStruct((rows, width), jnp.bfloat16),
        in_specs=[smem, smem, smem, vmem, vmem, pl.BlockSpec(memory_space=pltpu.HBM)],
        out_specs=vmem,
        scratch_shapes=[pltpu.VMEM(received.shape, jnp.bfloat16), pltpu.SemaphoreType.DMA],
        compiler_params=pltpu.CompilerParams(vmem_limit_bytes=24 * MIB),
        cost_estimate=pl.CostEstimate(
            flops=4 * rows * width * 1056 * 4, bytes_accessed=received.size * 2 + 4 * rows * width, transcendentals=rows * 8 * 1056
        ),
        name="attend",
    )(idx, lengths, above, queries, fresh, received)


def project_kernel(first, order_ref, attn_ref, w_ref, out_ref):
    count, rows, cols = out_ref.shape

    @pl.loop(0, count)
    def _(b):
        w = w_ref[:, pl.ds(pl.multiple_of(order_ref[b] * cols, cols), cols)]
        attn = attn_ref[first : first + rows, :]
        out_ref[b] = jnp.dot(attn, w, preferred_element_type=jnp.float32).astype(jnp.bfloat16)


def project(first, rows, order, attn, w_out):
    depth, width = w_out.shape
    cols = width // 8
    count = order.shape[0]
    smem = pl.BlockSpec(memory_space=pltpu.SMEM)
    vmem = pl.BlockSpec(memory_space=pltpu.VMEM)
    return pl.pallas_call(
        functools.partial(project_kernel, first),
        out_shape=jax.ShapeDtypeStruct((count, rows, cols), jnp.bfloat16),
        in_specs=[smem, vmem, vmem],
        out_specs=vmem,
        compiler_params=pltpu.CompilerParams(vmem_limit_bytes=24 * MIB),
        cost_estimate=pl.CostEstimate(
            flops=2 * rows * depth * cols * count, bytes_accessed=rows * cols * count * 2, transcendentals=0
        ),
        name="project",
    )(order, attn, w_out)


def shift(dy, dx):
    return [(s, (s // 4 + dy) % 4 * 4 + (s % 4 + dx) % 4) for s in range(RANKS)]


def turn(d):
    return [(t, (t + 2 * d) % 8) for t in range(8)]


def gather_row(fresh):
    mine = fresh[: ROOTS * NEW]
    return jnp.concatenate([mine] + [lax.ppermute(mine, "dp", shift(0, d)) for d in (1, 2, 3)], axis=0)


def above_of(parent, rank, nodes):
    own = lax.dynamic_slice_in_dim(parent, rank * nodes, nodes)
    child = jnp.arange(nodes, dtype=jnp.int32) - ROOTS
    source = jnp.maximum(own, 0) // nodes // 4 * 4 + child // SHARE
    row = (source * (PAIR + 1) + PAIR) * PAGE + child % SHARE * NEW
    return jnp.where((own >= 0) & (child >= 0), row, -1)


def slots_of(table, ranks, pages_dev):
    owner = table // pages_dev
    page = jnp.arange(ranks * pages_dev, dtype=jnp.int32)
    present = jnp.any(table[None, :] == page[:, None], axis=1)
    place = jnp.sum(
        (present[None, :] & (page[None, :] // pages_dev == owner[:, None]) & (page[None, :] < table[:, None])).astype(jnp.int32),
        axis=1,
    )
    return owner * (PAIR + 1) + place


def sum_over_tensor(kept, back):
    def pair(i):
        return kept[i].astype(jnp.float32) + back[i].astype(jnp.float32)

    half = kept.shape[1] // 2
    far = pair(2).astype(jnp.bfloat16)
    from_low = lax.ppermute(far[:half], "tensor", turn(1)).astype(jnp.float32)
    from_high = lax.ppermute(far[half:], "tensor", turn(-1)).astype(jnp.float32)
    up, down = pair(1), pair(3)
    up = jnp.concatenate([up[:half] + from_low, up[half:]], axis=0).astype(jnp.bfloat16)
    down = jnp.concatenate([down[:half], down[half:] + from_high], axis=0).astype(jnp.bfloat16)
    return (
        pair(0)
        + lax.ppermute(up, "tensor", turn(1)).astype(jnp.float32)
        + lax.ppermute(down, "tensor", turn(-1)).astype(jnp.float32)
    )


def body(queries, fresh_kv, kv_pool, page_table, path_len, parent, w_out, residual, gain):
    rank = lax.axis_index("dp")
    tensor_rank = lax.axis_index("tensor")
    tensors = lax.axis_size("tensor")
    rows = queries.shape[0]
    nodes = rows // NEW
    pages_dev = kv_pool.shape[0]
    row = gather_row(fresh_kv)
    send = pack(rank.reshape(1), page_table.T, kv_pool)
    send = pack_parents(rank.reshape(1), parent, row, send)

    own_table = lax.dynamic_slice_in_dim(page_table, rank * nodes, nodes).reshape(-1)
    idx = slots_of(own_table, RANKS, pages_dev)
    lengths = lax.dynamic_slice_in_dim(path_len, rank * nodes, nodes)
    above = above_of(parent, rank, nodes)
    z, core = tensor_rank // 2, tensor_rank % 2
    around = (z + jnp.arange(4, dtype=jnp.int32)) % 4 * 2
    other, same = around + 1 - core, around + core

    send, idx, lengths, above, other, same = lax.optimization_barrier((send, idx, lengths, above, other, same))
    received = lax.all_to_all(send, "dp", split_axis=0, concat_axis=0, tiled=True)
    received, queries, fresh_kv, w_out, residual, gain = lax.optimization_barrier(
        (received, queries, fresh_kv, w_out, residual, gain)
    )
    received = received.reshape(RANKS * (PAIR + 1), PAGE, kv_pool.shape[2])
    attn = attend(idx, lengths, above, queries, fresh_kv, received)
    swap = [(t, t ^ 1) for t in range(tensors)]
    summed, first = [], 0
    for families in GROUPS:
        count = families * FAM * NEW
        away = project(first, count, other, attn, w_out)
        away, attn = lax.optimization_barrier((away, attn))
        back = lax.ppermute(away, "tensor", swap)
        kept = project(first, count, same, attn, w_out)
        kept, attn = lax.optimization_barrier((kept, attn))
        summed.append(sum_over_tensor(kept, back))
        first += count

    cols = summed[0].shape[1]
    mine = lax.dynamic_slice_in_dim(residual, tensor_rank * cols, cols, 1)
    mixed = mine.astype(jnp.float32) + jnp.concatenate(summed, axis=0)
    power = jnp.sum(mixed * mixed, axis=1).reshape(rows // 128, 128)
    power = power + lax.ppermute(power, "tensor", swap)
    total = power
    for d in (1, 2, 3):
        total = total + lax.ppermute(power, "tensor", turn(d))
    norm = lax.rsqrt(total.reshape(rows, 1) / D + 1e-05)
    own_gain = lax.dynamic_slice_in_dim(gain, tensor_rank * cols, cols)
    normed = mixed * norm * own_gain.astype(jnp.float32)
    return (mixed.astype(jnp.bfloat16), normed.astype(jnp.bfloat16))


def solution(mesh):
    return jax.shard_map(
        body,
        mesh=mesh,
        in_specs=(
            P("dp", "tensor"),
            P("dp", "tensor"),
            P("dp", None, "tensor"),
            P(),
            P(),
            P(),
            P("tensor", None),
            P("dp", None),
            P(),
        ),
        out_specs=(P("dp", "tensor"), P("dp", "tensor")),
        check_vma=False,
    )
```

```python
import functools

import jax
import jax.numpy as jnp
from jax import lax
from jax.experimental import pallas as pl
from jax.experimental.pallas import tpu as pltpu
from jax.sharding import PartitionSpec as P

D = 8192
HD = 128
NEW = 16
PAGE = 64
PATH_PAGES = 16
SHARED = 8
FAM = 4
RANKS = 16
PAIR = 15
ROOTS = 12
SHARE = 3
GROUPS = 2
LOG2E = 1.4426950408889634
MIB = 1024 * 1024


def pack_kernel(
    rank_ref,
    parent_hbm,
    table_hbm,
    pool_hbm,
    near0_ref,
    near1_ref,
    near2_ref,
    near3_ref,
    send_ref,
    parent_ref,
    table_ref,
    pool_ref,
    wanted_ref,
    wanted_smem,
    sems,
):
    pages_dev = pool_ref.shape[0]
    slots, nodes = table_ref.shape
    base = rank_ref[0] * pages_dev
    table_copy = pltpu.make_async_copy(table_hbm, table_ref, sems.at[0])
    parent_copy = pltpu.make_async_copy(parent_hbm, parent_ref, sems.at[1])
    pool_copy = pltpu.make_async_copy(pool_hbm, pool_ref, sems.at[2])
    table_copy.start()
    parent_copy.start()
    pool_copy.start()
    table_copy.wait()
    table = table_ref[...]
    height = -(-pages_dev // 16) * 16
    row = lax.broadcasted_iota(jnp.int32, (height, nodes), 0)
    hits = jnp.zeros((height, nodes), jnp.float32)
    for page in range(pages_dev):
        hit = jnp.max((table == base + page).astype(jnp.float32), axis=0, keepdims=True)
        hits = jnp.where(row == page, hit, hits)
    node = lax.broadcasted_iota(jnp.int32, (nodes, 128), 0)
    begin = lax.broadcasted_iota(jnp.int32, (nodes, 128), 1) * (nodes // RANKS)
    belongs = ((node >= begin) & (node < begin + nodes // RANKS)).astype(jnp.bfloat16)
    present = jnp.dot(hits.astype(jnp.bfloat16), belongs, preferred_element_type=jnp.float32) > 0
    low = lax.broadcasted_iota(jnp.int32, (height, height), 0)
    high = lax.broadcasted_iota(jnp.int32, (height, height), 1)
    before = jnp.dot(
        (high < low).astype(jnp.bfloat16), present.astype(jnp.bfloat16), preferred_element_type=jnp.float32
    )
    place = jnp.where(present, before, -1.0)
    page_id = lax.broadcasted_iota(jnp.int32, (height, 128), 0).astype(jnp.float32)
    line = lax.broadcasted_iota(jnp.int32, (16, 128), 0)
    wanted = jnp.zeros((16, 128), jnp.float32)
    for slot in range(PAIR):
        page = jnp.sum(jnp.where(place == slot, page_id, 0.0), axis=0, keepdims=True)
        wanted = jnp.where(line == slot, page, wanted)
    wanted_ref[...] = wanted.astype(jnp.int32)
    copy = pltpu.make_async_copy(wanted_ref, wanted_smem, sems.at[3])
    copy.start()
    parent_copy.wait()
    x = rank_ref[0] % 4
    per_rank = nodes // RANKS

    @pl.loop(0, RANKS)
    def _(dest):
        for i in range(SHARE):
            named = jnp.maximum(parent_ref[dest * per_rank + ROOTS + x * SHARE + i], 0)
            away = (x + 4 - named // per_rank % 4) % 4
            rows = pl.ds(pl.multiple_of(named % per_rank * NEW, NEW), NEW)
            picked = near0_ref[rows, :]
            for d, ref in ((1, near1_ref), (2, near2_ref), (3, near3_ref)):
                picked = jnp.where(away == d, ref[rows, :], picked)
            send_ref[dest, PAIR, i * NEW : (i + 1) * NEW, :] = picked

    copy.wait()
    pool_copy.wait()

    @pl.loop(0, RANKS)
    def _(dest):
        for slot in range(PAIR):
            page = jnp.clip(wanted_smem[slot, dest], 0, pages_dev - 1)
            send_ref[dest, slot] = pool_ref[page]


def pack(rank, parent, table, pool, near):
    smem = pl.BlockSpec(memory_space=pltpu.SMEM)
    vmem = pl.BlockSpec(memory_space=pltpu.VMEM)
    return pl.pallas_call(
        pack_kernel,
        out_shape=pltpu.VMEM((RANKS, PAIR + 1) + pool.shape[1:], pool.dtype),
        in_specs=[smem] + [pl.BlockSpec(memory_space=pltpu.HBM)] * 3 + [vmem] * 4,
        out_specs=vmem,
        scratch_shapes=[
            pltpu.SMEM(parent.shape, jnp.int32),
            pltpu.VMEM(table.shape, jnp.int32),
            pltpu.VMEM(pool.shape, pool.dtype),
            pltpu.VMEM((16, 128), jnp.int32),
            pltpu.SMEM((16, 128), jnp.int32),
            pltpu.SemaphoreType.DMA((4,)),
        ],
        compiler_params=pltpu.CompilerParams(vmem_limit_bytes=55 * MIB),
        name="pack",
    )(rank, parent, table, pool, *near)


def attend_family(first, node, idx_ref, len_ref, above_ref, q_ref, fresh_ref, pages_ref, attn_ref):
    scale = HD ** (-0.5) * LOG2E
    nt = (((1,), (1,)), ((), ()))

    def pages(n, slot):
        return jnp.concatenate([pages_ref[idx_ref[n * PATH_PAGES + slot + s]] for s in range(SHARED)], axis=0)

    heads = q_ref.shape[1] // HD
    span = heads * NEW
    shared = pages(node, 0)
    queries = []
    for i in range(FAM):
        rows = q_ref[first + i * NEW : first + (i + 1) * NEW, :]
        queries.append(jnp.concatenate([rows[:, h * HD : (h + 1) * HD] for h in range(heads)], axis=0))
    s_shared = lax.dot_general(
        jnp.concatenate(queries, axis=0), shared[:, :HD], nt, preferred_element_type=jnp.float32
    )
    half = SHARED * PAGE // 2
    own, s_own = [], []
    for i in range(FAM):
        above = above_ref[node + i]
        spot = jnp.maximum(above, 0)
        upper = pages_ref[spot // PAGE, pl.ds(pl.multiple_of(spot % PAGE, NEW), NEW), :]
        fresh = fresh_ref[first + i * NEW : first + (i + 1) * NEW, :]
        kv = jnp.concatenate([pages(node + i, SHARED), fresh, upper], axis=0)
        s = lax.dot_general(queries[i], kv[:, :HD], nt, preferred_element_type=jnp.float32)
        late = s[:, half:]
        spot = lax.broadcasted_iota(jnp.int32, late.shape, 1) + SHARED * PAGE + half
        token = lax.broadcasted_iota(jnp.int32, late.shape, 0) % NEW
        key = spot - PATH_PAGES * PAGE
        limit = jnp.where(above >= 0, 2 * NEW, NEW)
        allowed = (spot < len_ref[node + i]) | ((key >= 0) & (key <= token)) | ((key >= NEW) & (key < limit))
        own.append(kv)
        s_own.append(jnp.concatenate([s[:, :half], jnp.where(allowed, late, -jnp.inf)], axis=1))
    tops = [
        jnp.maximum(
            jnp.max(s_shared[i * span : (i + 1) * span], axis=1, keepdims=True),
            jnp.max(s_own[i], axis=1, keepdims=True),
        )
        for i in range(FAM)
    ]
    w_own = [jnp.exp2((s_own[i] - tops[i]) * scale).astype(jnp.bfloat16) for i in range(FAM)]
    w_shared = jnp.exp2((s_shared - jnp.concatenate(tops, axis=0)) * scale).astype(jnp.bfloat16)
    ones = jnp.ones((own[0].shape[0], HD), jnp.bfloat16)
    accum = [
        jnp.dot(w_own[i], jnp.concatenate([own[i][:, HD:], ones], axis=1), preferred_element_type=jnp.float32)
        for i in range(FAM)
    ]
    accum = jnp.concatenate(accum, axis=0) + jnp.dot(
        w_shared, jnp.concatenate([shared[:, HD:], ones[: SHARED * PAGE]], axis=1), preferred_element_type=jnp.float32
    )
    attn = (accum[:, :HD] / accum[:, HD:]).astype(jnp.bfloat16)
    for i in range(FAM):
        for h in range(heads):
            block = attn[i * span + h * NEW : i * span + (h + 1) * NEW, :]
            attn_ref[first + i * NEW : first + (i + 1) * NEW, h * HD : (h + 1) * HD] = block


def attend_kernel(idx_ref, len_ref, above_ref, q_ref, fresh_ref, pages_ref, attn_ref):
    for f in range(q_ref.shape[0] // (FAM * NEW)):
        attend_family(f * FAM * NEW, f * FAM, idx_ref, len_ref, above_ref, q_ref, fresh_ref, pages_ref, attn_ref)


def attend(idx, lengths, above, queries, fresh, received):
    rows, width = queries.shape
    smem = pl.BlockSpec(memory_space=pltpu.SMEM)
    vmem = pl.BlockSpec(memory_space=pltpu.VMEM)
    return pl.pallas_call(
        attend_kernel,
        out_shape=jax.ShapeDtypeStruct((rows, width), jnp.bfloat16),
        in_specs=[smem, smem, smem, vmem, vmem, vmem],
        out_specs=vmem,
        compiler_params=pltpu.CompilerParams(vmem_limit_bytes=24 * MIB),
        cost_estimate=pl.CostEstimate(
            flops=4 * rows * width * 1056 * 4, bytes_accessed=received.size * 2 + 4 * rows * width, transcendentals=rows * 8 * 1056
        ),
        name="attend",
    )(idx, lengths, above, queries, fresh, received)


def project_kernel(order_ref, attn_ref, w_ref, out_ref):
    count, rows, cols = out_ref.shape

    @pl.loop(0, count)
    def _(b):
        w = w_ref[:, pl.ds(pl.multiple_of(order_ref[b] * cols, cols), cols)]
        out_ref[b] = jnp.dot(attn_ref[...], w, preferred_element_type=jnp.float32).astype(jnp.bfloat16)


def project(order, attn, w_out):
    rows, depth = attn.shape
    cols = w_out.shape[1] // 8
    count = order.shape[0]
    smem = pl.BlockSpec(memory_space=pltpu.SMEM)
    vmem = pl.BlockSpec(memory_space=pltpu.VMEM)
    return pl.pallas_call(
        project_kernel,
        out_shape=jax.ShapeDtypeStruct((count, rows, cols), jnp.bfloat16),
        in_specs=[smem, vmem, vmem],
        out_specs=vmem,
        compiler_params=pltpu.CompilerParams(vmem_limit_bytes=12 * MIB),
        cost_estimate=pl.CostEstimate(
            flops=2 * rows * depth * cols * count, bytes_accessed=rows * cols * count * 2, transcendentals=0
        ),
        name="project",
    )(order, attn, w_out)


def shift(dy, dx):
    return [(s, (s // 4 + dy) % 4 * 4 + (s % 4 + dx) % 4) for s in range(RANKS)]


def turn(d):
    return [(t, (t + 2 * d) % 8) for t in range(8)]


def above_of(parent, rank, nodes):
    own = lax.dynamic_slice_in_dim(parent, rank * nodes, nodes)
    child = jnp.arange(nodes, dtype=jnp.int32) - ROOTS
    source = jnp.maximum(own, 0) // nodes // 4 * 4 + child // SHARE
    row = (source * (PAIR + 1) + PAIR) * PAGE + child % SHARE * NEW
    return jnp.where((own >= 0) & (child >= 0), row, -1)


def slots_of(table, ranks, pages_dev):
    owner = table // pages_dev
    page = jnp.arange(ranks * pages_dev, dtype=jnp.int32)
    present = jnp.any(table[None, :] == page[:, None], axis=1)
    place = jnp.sum(
        (present[None, :] & (page[None, :] // pages_dev == owner[:, None]) & (page[None, :] < table[:, None])).astype(jnp.int32),
        axis=1,
    )
    return owner * (PAIR + 1) + place


def far_kernel(kept_ref, back_ref, *out_refs):
    rows = out_refs[0].shape[0]
    for i, ref in enumerate(out_refs):
        part = pl.ds(i * rows, rows)
        ref[...] = (kept_ref[1, part].astype(jnp.float32) + back_ref[part].astype(jnp.float32)).astype(jnp.bfloat16)


def near_kernel(first, kept_ref, back_ref, from_low_ref, from_high_ref, up_ref, down_ref):
    half = from_low_ref.shape[0]
    low, high = pl.ds(0, half), pl.ds(half, half)

    def pair(i, start):
        part = pl.ds(first + start, half)
        return kept_ref[i, part].astype(jnp.float32) + back_ref[i, part].astype(jnp.float32)

    up_ref[low] = (pair(0, 0) + from_low_ref[...].astype(jnp.float32)).astype(jnp.bfloat16)
    up_ref[high] = pair(0, half).astype(jnp.bfloat16)
    down_ref[low] = pair(1, 0).astype(jnp.bfloat16)
    down_ref[high] = (pair(1, half) + from_high_ref[...].astype(jnp.float32)).astype(jnp.bfloat16)


def last_kernel(first, kept_ref, back_ref, up_ref, down_ref, residual_ref, mixed_ref, power_ref):
    part = pl.ds(first, up_ref.shape[0])
    mixed = residual_ref[part].astype(jnp.float32)
    for term in (kept_ref[2, part], back_ref[2, part], up_ref[...], down_ref[...]):
        mixed = mixed + term.astype(jnp.float32)
    mixed_ref[...] = mixed
    power_ref[...] = lax.dot_general(
        jnp.ones((8, mixed.shape[1]), jnp.float32),
        mixed * mixed,
        (((1,), (1,)), ((), ())),
        precision=lax.Precision.HIGHEST,
        preferred_element_type=jnp.float32,
    )


def local(kernel, name, outs, *args):
    vmem = pl.BlockSpec(memory_space=pltpu.VMEM)
    return pl.pallas_call(
        kernel,
        out_shape=[jax.ShapeDtypeStruct(shape, dtype) for shape, dtype in outs],
        in_specs=[vmem] * len(args),
        out_specs=[vmem] * len(outs),
        compiler_params=pltpu.CompilerParams(vmem_limit_bytes=12 * MIB),
        name=name,
    )(*args)


def body(queries, fresh_kv, kv_pool, page_table, path_len, parent, w_out, residual, gain):
    rank = lax.axis_index("dp")
    tensor_rank = lax.axis_index("tensor")
    tensors = lax.axis_size("tensor")
    rows = queries.shape[0]
    nodes = rows // NEW
    pages_dev = kv_pool.shape[0]
    roots = fresh_kv[: ROOTS * NEW]
    near = [roots] + [lax.ppermute(roots, "dp", shift(0, d)) for d in (1, 2, 3)]
    send = pack(rank.reshape(1), parent, page_table.T, kv_pool, near)

    own_table = lax.dynamic_slice_in_dim(page_table, rank * nodes, nodes).reshape(-1)
    idx = slots_of(own_table, RANKS, pages_dev)
    lengths = lax.dynamic_slice_in_dim(path_len, rank * nodes, nodes)
    above = above_of(parent, rank, nodes)
    z, core = tensor_rank // 2, tensor_rank % 2
    far, rest = (z + 2) % 4 * 2, (z + jnp.array([1, 3, 0], jnp.int32)) % 4 * 2
    far = jnp.stack([far + 1 - core, far + core])
    other, same = rest + 1 - core, rest + core

    send, idx, lengths, above, far, other, same = lax.optimization_barrier((send, idx, lengths, above, far, other, same))
    received = lax.all_to_all(send, "dp", split_axis=0, concat_axis=0, tiled=True)
    received, queries, fresh_kv, w_out, residual, gain = lax.optimization_barrier(
        (received, queries, fresh_kv, w_out, residual, gain)
    )
    received = received.reshape(RANKS * (PAIR + 1), PAGE, kv_pool.shape[2])
    attn = attend(idx, lengths, above, queries, fresh_kv, received)

    swap = [(t, t ^ 1) for t in range(tensors)]
    cols = D // tensors
    mine = lax.dynamic_slice_in_dim(residual, tensor_rank * cols, cols, 1)
    group = rows // GROUPS
    both = project(far, attn, w_out)
    both, attn = lax.optimization_barrier((both, attn))
    far_back = lax.ppermute(both[0], "tensor", swap)
    away = project(other, attn, w_out)
    far_back, away, attn = lax.optimization_barrier((far_back, away, attn))
    back = lax.ppermute(away, "tensor", swap)
    halves = [((group // 2, cols), jnp.bfloat16)] * (2 * GROUPS)
    sent = local(far_kernel, "far", halves, both, far_back)
    *sent, attn = lax.optimization_barrier((*sent, attn))
    low = [lax.ppermute(sent[2 * g], "tensor", turn(1)) for g in range(GROUPS)]
    high = [lax.ppermute(sent[2 * g + 1], "tensor", turn(-1)) for g in range(GROUPS)]
    kept = project(same, attn, w_out)
    whole = ((group, cols), jnp.bfloat16)
    ups, downs = [], []
    for g in range(GROUPS):
        up, down = local(
            functools.partial(near_kernel, g * group), "near", [whole, whole], kept, back, low[g], high[g]
        )
        ups.append(lax.ppermute(up, "tensor", turn(1)))
        downs.append(lax.ppermute(down, "tensor", turn(-1)))
    outs = [((group, cols), jnp.float32), ((8, group), jnp.float32)]
    done = [
        local(functools.partial(last_kernel, g * group), "last", outs, kept, back, ups[g], downs[g], mine)
        for g in range(GROUPS)
    ]

    mixed = jnp.concatenate([m for m, _ in done], axis=0)
    power = jnp.concatenate([p for _, p in done], axis=1)
    power = power + lax.ppermute(power, "tensor", swap)
    total = power
    for d in (1, 2, 3):
        total = total + lax.ppermute(power, "tensor", turn(d))
    norm = lax.rsqrt(total[0].reshape(rows, 1) / D + 1e-05)
    own_gain = lax.dynamic_slice_in_dim(gain, tensor_rank * cols, cols)
    normed = mixed * norm * own_gain.astype(jnp.float32)
    return (mixed.astype(jnp.bfloat16), normed.astype(jnp.bfloat16))


def solution(mesh):
    return jax.shard_map(
        body,
        mesh=mesh,
        in_specs=(
            P("dp", "tensor"),
            P("dp", "tensor"),
            P("dp", None, "tensor"),
            P(),
            P(),
            P(),
            P("tensor", None),
            P("dp", None),
            P(),
        ),
        out_specs=(P("dp", "tensor"), P("dp", "tensor")),
        check_vma=False,
    )
```

```python
import functools

import jax
import jax.numpy as jnp
from jax import lax
from jax.experimental import pallas as pl
from jax.experimental.pallas import tpu as pltpu
from jax.sharding import PartitionSpec as P

D = 8192
HD = 128
NEW = 16
PAGE = 64
PATH_PAGES = 16
SHARED = 8
FAM = 4
RANKS = 16
PAIR = 15
ROOTS = 12
EXTRA = 3
NEAR = (0, 1, 3)
GROUPS = 2
LOG2E = 1.4426950408889634
MIB = 1024 * 1024


def split_kernel(pool_ref, fresh_ref, *refs):
    outs, sem = refs[:-1], refs[-1]
    pages_dev = pool_ref.shape[0]
    for i, out in enumerate(outs):
        lanes = pl.ds(i * HD, HD)
        pltpu.make_async_copy(pool_ref.at[:, :, lanes], out.at[pl.ds(0, pages_dev)], sem.at[i]).start()
        for p in range(EXTRA):
            rows = pl.ds(p * PAGE, PAGE)
            pltpu.make_async_copy(fresh_ref.at[rows, lanes], out.at[pages_dev + p], sem.at[i]).start()
    for i, out in enumerate(outs):
        pltpu.make_async_copy(out, out, sem.at[i]).wait()


def split(pool, fresh):
    hbm = pl.BlockSpec(memory_space=pltpu.HBM)
    vmem = pl.BlockSpec(memory_space=pltpu.VMEM)
    part = jax.ShapeDtypeStruct((pool.shape[0] + EXTRA, PAGE, HD), pool.dtype)
    return pl.pallas_call(
        split_kernel,
        out_shape=[part, part],
        in_specs=[hbm, hbm],
        out_specs=[vmem, vmem],
        scratch_shapes=[pltpu.SemaphoreType.DMA((2,))],
        compiler_params=pltpu.CompilerParams(vmem_limit_bytes=55 * MIB),
        name="split",
    )(pool, fresh)


def plan_kernel(pages_dev, rank_ref, table_ref, wanted_ref):
    rank = rank_ref[0]
    y, x = rank // 4, rank % 4
    slots, nodes = table_ref.shape
    table = table_ref[...]
    height = -(-pages_dev // 16) * 16
    per_rank = nodes // RANKS
    row = lax.broadcasted_iota(jnp.int32, (height, nodes), 0)
    node = lax.broadcasted_iota(jnp.int32, (nodes, 128), 0)
    column = lax.broadcasted_iota(jnp.int32, (nodes, 128), 1)
    step = column & 3
    begin = jnp.where(column < 16, ((y + step) & 3) * 4 + x, y * 4 + ((x + step) & 3)) * per_rank
    belongs = (node >= begin) & (node < begin + per_rank)
    low = lax.broadcasted_iota(jnp.int32, (height, height), 0)
    high = lax.broadcasted_iota(jnp.int32, (height, height), 1)
    earlier = (high < low).astype(jnp.bfloat16)
    page_id = lax.broadcasted_iota(jnp.int32, (height, 128), 0).astype(jnp.float32)
    line = lax.broadcasted_iota(jnp.int32, (16, 128), 0)
    wanted_ref[...] = jnp.zeros((16, 128), jnp.int32)

    @pl.loop(0, 8)
    def _(part):
        back = part % 4
        owner = jnp.where(part < 4, y * 4 + (x + 4 - back) % 4, (y + 4 - back) % 4 * 4 + x)
        base = owner * pages_dev
        hits = jnp.zeros((height, nodes), jnp.float32)
        for page in range(pages_dev):
            hit = jnp.max((table == base + page).astype(jnp.float32), axis=0, keepdims=True)
            hits = jnp.where(row == page, hit, hits)
        mine = (belongs & (column // 4 == part)).astype(jnp.bfloat16)
        present = jnp.dot(hits.astype(jnp.bfloat16), mine, preferred_element_type=jnp.float32) > 0
        before = jnp.dot(earlier, present.astype(jnp.bfloat16), preferred_element_type=jnp.float32)
        place = jnp.where(present, before, -1.0)
        wanted = jnp.zeros((16, 128), jnp.float32)
        for slot in range(PAIR):
            page = jnp.sum(jnp.where(place == slot, page_id, 0.0), axis=0, keepdims=True)
            wanted = jnp.where(line == slot, page, wanted)
        wanted_ref[...] += wanted.astype(jnp.int32)


def plan(rank, table, pages_dev):
    vmem = pl.BlockSpec(memory_space=pltpu.VMEM)
    return pl.pallas_call(
        functools.partial(plan_kernel, pages_dev),
        out_shape=jax.ShapeDtypeStruct((16, 128), jnp.int32),
        in_specs=[pl.BlockSpec(memory_space=pltpu.SMEM), vmem],
        out_specs=vmem,
        name="plan",
    )(rank, table)


def copy_pages(out, first, ref, wanted_ref, column, pages_dev):
    for slot in range(PAIR):
        page = jnp.clip(wanted_ref[slot, column], 0, pages_dev - 1)
        out[first + slot] = ref[page]


def pack_first_kernel(pages_dev, wanted_ref, *refs):
    for i in range(2):
        parts, outs = refs[3 * i : 3 * i + 3], refs[6 + 4 * i : 10 + 4 * i]
        for e, out in enumerate(outs):
            for j, d in enumerate(NEAR):
                copy_pages(out, j * PAIR, parts[j], wanted_ref, 16 * i + 4 * d + e, pages_dev)


def pack_first(wanted, pages_dev, keys, values):
    outs = [((len(NEAR) * PAIR, PAGE, HD), jnp.bfloat16)] * 8
    args = [keys[d] for d in NEAR] + [values[d] for d in NEAR]
    return local(functools.partial(pack_first_kernel, pages_dev), "pack_first", outs, wanted, *args, scalars=1, limit=62)


def pack_second_kernel(pages_dev, rank_ref, parent_ref, wanted_ref, *refs):
    y, x = rank_ref[0] // 4, rank_ref[0] % 4
    per_rank = parent_ref.shape[0] // RANKS
    for i in range(2):
        parts, outs = refs[4 * i : 4 * i + 4], refs[8 + 4 * i : 12 + 4 * i]
        for e, out in enumerate(outs):
            copy_pages(out, 0, parts[2], wanted_ref, 16 * i + 8 + e, pages_dev)
            dest = (y + e) % 4 * 4 + x if i == 0 else y * 4 + (x + e) % 4
            for child in range(per_rank - ROOTS):
                named = jnp.maximum(parent_ref[dest * per_rank + ROOTS + child], 0)
                up = named // per_rank
                away = (x + 4 - up % 4) % 4 if i == 0 else (y + 4 - up // 4) % 4
                root = jnp.minimum(named % per_rank, ROOTS - 1)
                page, rows = pages_dev + root // 4, pl.ds(pl.multiple_of(root % 4 * NEW, NEW), NEW)
                picked = parts[0][page, rows, :]
                for d in (1, 2, 3):
                    picked = jnp.where(away == d, parts[d][page, rows, :], picked)
                out[PAIR + child // 4, child % 4 * NEW : (child % 4 + 1) * NEW, :] = picked


def pack_second(rank, parent, wanted, pages_dev, keys, values):
    outs = [((PAIR + EXTRA, PAGE, HD), jnp.bfloat16)] * 8
    kernel = functools.partial(pack_second_kernel, pages_dev)
    return local(kernel, "pack_second", outs, rank, parent, wanted, *keys, *values, scalars=3, limit=62)


def attend_family(first, node, at_refs, len_ref, above_refs, q_ref, fresh_ref, page_refs, attn_ref):
    scale = HD ** (-0.5) * LOG2E
    nt = (((1,), (1,)), ((), ()))

    def pages(i, n, slot):
        return [page_refs[i][at_refs[i][n * PATH_PAGES + slot + s]] for s in range(SHARED)]

    heads = q_ref.shape[1] // HD
    span = heads * NEW
    shared_key, shared_value = [jnp.concatenate(pages(i, node, 0), axis=0) for i in range(2)]
    queries = []
    for i in range(FAM):
        rows = q_ref[first + i * NEW : first + (i + 1) * NEW, :]
        queries.append(jnp.concatenate([rows[:, h * HD : (h + 1) * HD] for h in range(heads)], axis=0))
    s_shared = lax.dot_general(
        jnp.concatenate(queries, axis=0), shared_key, nt, preferred_element_type=jnp.float32
    )
    half = SHARED * PAGE // 2
    values, s_own = [], []
    for i in range(FAM):
        both = []
        for j in range(2):
            spot = jnp.maximum(above_refs[j][node + i], 0)
            upper = page_refs[j][spot // PAGE, pl.ds(pl.multiple_of(spot % PAGE, NEW), NEW), :]
            fresh = fresh_ref[first + i * NEW : first + (i + 1) * NEW, j * HD : (j + 1) * HD]
            both.append(jnp.concatenate(pages(j, node + i, SHARED) + [fresh, upper], axis=0))
        s = lax.dot_general(queries[i], both[0], nt, preferred_element_type=jnp.float32)
        late = s[:, half:]
        spot = lax.broadcasted_iota(jnp.int32, late.shape, 1) + SHARED * PAGE + half
        token = lax.broadcasted_iota(jnp.int32, late.shape, 0) % NEW
        key = spot - PATH_PAGES * PAGE
        limit = jnp.where(above_refs[0][node + i] >= 0, 2 * NEW, NEW)
        allowed = (spot < len_ref[node + i]) | ((key >= 0) & (key <= token)) | ((key >= NEW) & (key < limit))
        values.append(both[1])
        s_own.append(jnp.concatenate([s[:, :half], jnp.where(allowed, late, -jnp.inf)], axis=1))
    tops = [
        jnp.maximum(
            jnp.max(s_shared[i * span : (i + 1) * span], axis=1, keepdims=True),
            jnp.max(s_own[i], axis=1, keepdims=True),
        )
        for i in range(FAM)
    ]
    w_own = [jnp.exp2((s_own[i] - tops[i]) * scale).astype(jnp.bfloat16) for i in range(FAM)]
    w_shared = jnp.exp2((s_shared - jnp.concatenate(tops, axis=0)) * scale).astype(jnp.bfloat16)
    ones = jnp.ones((values[0].shape[0], HD), jnp.bfloat16)
    accum = [
        jnp.dot(w_own[i], jnp.concatenate([values[i], ones], axis=1), preferred_element_type=jnp.float32)
        for i in range(FAM)
    ]
    accum = jnp.concatenate(accum, axis=0) + jnp.dot(
        w_shared, jnp.concatenate([shared_value, ones[: SHARED * PAGE]], axis=1), preferred_element_type=jnp.float32
    )
    attn = (accum[:, :HD] / accum[:, HD:]).astype(jnp.bfloat16)
    for i in range(FAM):
        for h in range(heads):
            block = attn[i * span + h * NEW : i * span + (h + 1) * NEW, :]
            attn_ref[first + i * NEW : first + (i + 1) * NEW, h * HD : (h + 1) * HD] = block


def attend_kernel(*refs):
    at_refs, len_ref, above_refs, (q_ref, fresh_ref) = refs[:2], refs[2], refs[3:5], refs[5:7]
    sources, w_hbm, (attn_ref, w_ref), page_refs, sems = (refs[7:15], refs[15:23]), refs[23], refs[24:26], refs[26:28], refs[28]
    for i in range(2):
        start = 0
        for ref in sources[i]:
            count = ref.shape[0]
            pltpu.make_async_copy(ref, page_refs[i].at[pl.ds(start, count)], sems.at[i]).start()
            start += count
    weights = []
    for part in range(8):
        rows = pl.ds(part * (w_ref.shape[0] // 8), w_ref.shape[0] // 8)
        weights.append(pltpu.make_async_copy(w_hbm.at[rows], w_ref.at[rows], sems.at[2 + part]))
        weights[-1].start()
    for i in range(2):
        pltpu.make_async_copy(page_refs[i], page_refs[i], sems.at[i]).wait()
    for f in range(q_ref.shape[0] // (FAM * NEW)):
        attend_family(f * FAM * NEW, f * FAM, at_refs, len_ref, above_refs, q_ref, fresh_ref, page_refs, attn_ref)
    for copy in weights:
        copy.wait()


def attend(at, lengths, above, queries, fresh, keys, values, w_out):
    rows, width = queries.shape
    smem = pl.BlockSpec(memory_space=pltpu.SMEM)
    vmem = pl.BlockSpec(memory_space=pltpu.VMEM)
    hbm = pl.BlockSpec(memory_space=pltpu.HBM)
    pages = pltpu.VMEM((sum(k.shape[0] for k in keys), PAGE, HD), jnp.bfloat16)
    return pl.pallas_call(
        attend_kernel,
        out_shape=[jax.ShapeDtypeStruct((rows, width), jnp.bfloat16), pltpu.VMEM(w_out.shape, w_out.dtype)],
        in_specs=[smem] * 5 + [vmem] * 2 + [hbm] * 17,
        out_specs=[vmem, vmem],
        scratch_shapes=[pages, pages, pltpu.SemaphoreType.DMA((10,))],
        compiler_params=pltpu.CompilerParams(vmem_limit_bytes=45 * MIB),
        cost_estimate=pl.CostEstimate(
            flops=4 * rows * width * 1056 * 4, bytes_accessed=4 * rows * width, transcendentals=rows * 8 * 1056
        ),
        name="attend",
    )(*at, lengths, *above, queries, fresh, *keys, *values, w_out)


def project_kernel(order_ref, attn_ref, w_ref, out_ref):
    count, rows, cols = out_ref.shape

    @pl.loop(0, count)
    def _(b):
        w = w_ref[:, pl.ds(pl.multiple_of(order_ref[b] * cols, cols), cols)]
        out_ref[b] = jnp.dot(attn_ref[...], w, preferred_element_type=jnp.float32).astype(jnp.bfloat16)


def project(order, attn, w_out):
    rows, depth = attn.shape
    cols = w_out.shape[1] // 8
    count = order.shape[0]
    smem = pl.BlockSpec(memory_space=pltpu.SMEM)
    vmem = pl.BlockSpec(memory_space=pltpu.VMEM)
    return pl.pallas_call(
        project_kernel,
        out_shape=jax.ShapeDtypeStruct((count, rows, cols), jnp.bfloat16),
        in_specs=[smem, vmem, vmem],
        out_specs=vmem,
        compiler_params=pltpu.CompilerParams(vmem_limit_bytes=12 * MIB),
        cost_estimate=pl.CostEstimate(
            flops=2 * rows * depth * cols * count, bytes_accessed=rows * cols * count * 2, transcendentals=0
        ),
        name="project",
    )(order, attn, w_out)


def shift(dy, dx):
    return [(s, (s // 4 + dy) % 4 * 4 + (s % 4 + dx) % 4) for s in range(RANKS)]


def turn(d):
    return [(t, (t + 2 * d) % 8) for t in range(8)]


def places_of(table, path_parent, rank, pages_dev, nodes):
    owner = table // pages_dev
    other, mine = table[None, :], table[:, None]
    slot = jnp.arange(table.shape[0], dtype=jnp.int32)
    first = (slot % PATH_PAGES >= SHARED) | (slot // PATH_PAGES % FAM == 0)
    before = (other < mine) & (other >= (owner * pages_dev)[:, None]) & first[None, :]
    place = jnp.sum(before.astype(jnp.int32), axis=1)
    child = jnp.arange(nodes, dtype=jnp.int32) - ROOTS
    up = jnp.maximum(path_parent, 0) // nodes
    many, few = len(NEAR) * PAIR, PAIR + EXTRA

    def turns(r):
        return (rank // 4 - r // 4) % 4, (rank % 4 - r % 4) % 4

    at, above = [], []
    for i in range(2):
        e, d = turns(owner)[:: 1 - 2 * i]
        at.append(jnp.where(d == 2, 4 * many + e * few, e * many + jnp.minimum(d, 2) * PAIR) + place)
        row = (4 * many + turns(up)[i] * few + PAIR) * PAGE + child * NEW
        above.append(jnp.where((path_parent >= 0) & (child >= 0), row, -1))
    return at, above


def far_kernel(kept_ref, back_ref, *out_refs):
    rows = out_refs[0].shape[0]
    for i, ref in enumerate(out_refs):
        part = pl.ds(i * rows, rows)
        ref[...] = (kept_ref[1, part].astype(jnp.float32) + back_ref[part].astype(jnp.float32)).astype(jnp.bfloat16)


def near_kernel(first, kept_ref, back_ref, from_low_ref, from_high_ref, up_ref, down_ref):
    half = from_low_ref.shape[0]
    low, high = pl.ds(0, half), pl.ds(half, half)

    def pair(i, start):
        part = pl.ds(first + start, half)
        return kept_ref[i, part].astype(jnp.float32) + back_ref[i, part].astype(jnp.float32)

    up_ref[low] = (pair(0, 0) + from_low_ref[...].astype(jnp.float32)).astype(jnp.bfloat16)
    up_ref[high] = pair(0, half).astype(jnp.bfloat16)
    down_ref[low] = pair(1, 0).astype(jnp.bfloat16)
    down_ref[high] = (pair(1, half) + from_high_ref[...].astype(jnp.float32)).astype(jnp.bfloat16)


def last_kernel(first, kept_ref, back_ref, up_ref, down_ref, residual_ref, mixed_ref, power_ref):
    part = pl.ds(first, up_ref.shape[0])
    mixed = residual_ref[part].astype(jnp.float32)
    for term in (kept_ref[2, part], back_ref[2, part], up_ref[...], down_ref[...]):
        mixed = mixed + term.astype(jnp.float32)
    mixed_ref[...] = mixed
    power_ref[...] = lax.dot_general(
        jnp.ones((8, mixed.shape[1]), jnp.float32),
        mixed * mixed,
        (((1,), (1,)), ((), ())),
        precision=lax.Precision.HIGHEST,
        preferred_element_type=jnp.float32,
    )


def local(kernel, name, outs, *args, scalars=0, limit=12):
    vmem = pl.BlockSpec(memory_space=pltpu.VMEM)
    smem = pl.BlockSpec(memory_space=pltpu.SMEM)
    return pl.pallas_call(
        kernel,
        out_shape=[jax.ShapeDtypeStruct(shape, dtype) for shape, dtype in outs],
        in_specs=[smem] * scalars + [vmem] * (len(args) - scalars),
        out_specs=[vmem] * len(outs),
        compiler_params=pltpu.CompilerParams(vmem_limit_bytes=limit * MIB),
        name=name,
    )(*args)


def body(queries, fresh_kv, kv_pool, page_table, path_len, parent, w_out, residual, gain):
    rank = lax.axis_index("dp")
    tensor_rank = lax.axis_index("tensor")
    tensors = lax.axis_size("tensor")
    rows = queries.shape[0]
    nodes = rows // NEW
    pages_dev = kv_pool.shape[0]
    key, value = split(kv_pool, fresh_kv)
    place = rank.reshape(1)
    wanted = plan(place, page_table.T, pages_dev)
    far_key, far_value, wanted = lax.optimization_barrier((key, value, wanted))
    keys = [key] + [lax.ppermute(far_key if d == 2 else key, "dp", shift(0, d)) for d in (1, 2, 3)]
    values = [value] + [lax.ppermute(far_value if d == 2 else value, "dp", shift(d, 0)) for d in (1, 2, 3)]
    first = pack_first(wanted, pages_dev, keys, values)

    def deliver(parts):
        order = [(e, i) for e in (1, 3, 2) for i in range(2)]
        return {(i, e): lax.ppermute(parts[4 * i + e], "dp", shift(0, e) if i else shift(e, 0)) for e, i in order}

    got = deliver(first)
    got[0, 1], wanted = lax.optimization_barrier((got[0, 1], wanted))
    second = list(pack_second(place, parent, wanted, pages_dev, keys, values))
    for i, e in got:
        if (i, e) != (0, 1):
            got[i, e], second[4 * i + e] = lax.optimization_barrier((got[i, e], second[4 * i + e]))
    more = deliver(second)
    keys, values = (
        [first[4 * i]] + [got[i, e] for e in (1, 2, 3)] + [second[4 * i]] + [more[i, e] for e in (1, 2, 3)]
        for i in range(2)
    )
    keys, values, w_out, residual, gain = lax.optimization_barrier((keys, values, w_out, residual, gain))

    own_table = lax.dynamic_slice_in_dim(page_table, rank * nodes, nodes).reshape(-1)
    lengths = lax.dynamic_slice_in_dim(path_len, rank * nodes, nodes)
    at, above = places_of(own_table, lax.dynamic_slice_in_dim(parent, rank * nodes, nodes), rank, pages_dev, nodes)
    z, core = tensor_rank // 2, tensor_rank % 2
    far, rest = (z + 2) % 4 * 2, (z + jnp.array([1, 3, 0], jnp.int32)) % 4 * 2
    far = jnp.stack([far + 1 - core, far + core])
    other, same = rest + 1 - core, rest + core

    attn, w_held = attend(at, lengths, above, queries, fresh_kv, keys, values, w_out)

    swap = [(t, t ^ 1) for t in range(tensors)]
    cols = D // tensors
    mine = lax.dynamic_slice_in_dim(residual, tensor_rank * cols, cols, 1)
    group = rows // GROUPS
    both = project(far, attn, w_held)
    both, attn = lax.optimization_barrier((both, attn))
    far_back = lax.ppermute(both[0], "tensor", swap)
    away = project(other, attn, w_held)
    far_back, away, attn = lax.optimization_barrier((far_back, away, attn))
    back = lax.ppermute(away, "tensor", swap)
    halves = [((group // 2, cols), jnp.bfloat16)] * (2 * GROUPS)
    sent = local(far_kernel, "far", halves, both, far_back)
    *sent, attn = lax.optimization_barrier((*sent, attn))
    low = [lax.ppermute(sent[2 * g], "tensor", turn(1)) for g in range(GROUPS)]
    high = [lax.ppermute(sent[2 * g + 1], "tensor", turn(-1)) for g in range(GROUPS)]
    kept = project(same, attn, w_held)
    whole = ((group, cols), jnp.bfloat16)
    ups, downs = [], []
    for g in range(GROUPS):
        up, down = local(
            functools.partial(near_kernel, g * group), "near", [whole, whole], kept, back, low[g], high[g]
        )
        ups.append(lax.ppermute(up, "tensor", turn(1)))
        downs.append(lax.ppermute(down, "tensor", turn(-1)))
    outs = [((group, cols), jnp.float32), ((8, group), jnp.float32)]
    done = [
        local(functools.partial(last_kernel, g * group), "last", outs, kept, back, ups[g], downs[g], mine)
        for g in range(GROUPS)
    ]

    mixed = jnp.concatenate([m for m, _ in done], axis=0)
    power = jnp.concatenate([p for _, p in done], axis=1)
    power = power + lax.ppermute(power, "tensor", swap)
    total = power
    for d in (1, 2, 3):
        total = total + lax.ppermute(power, "tensor", turn(d))
    norm = lax.rsqrt(total[0].reshape(rows, 1) / D + 1e-05)
    own_gain = lax.dynamic_slice_in_dim(gain, tensor_rank * cols, cols)
    normed = mixed * norm * own_gain.astype(jnp.float32)
    return (mixed.astype(jnp.bfloat16), normed.astype(jnp.bfloat16))


def solution(mesh):
    return jax.shard_map(
        body,
        mesh=mesh,
        in_specs=(
            P("dp", "tensor"),
            P("dp", "tensor"),
            P("dp", None, "tensor"),
            P(),
            P(),
            P(),
            P("tensor", None),
            P("dp", None),
            P(),
        ),
        out_specs=(P("dp", "tensor"), P("dp", "tensor")),
        check_vma=False,
    )
```

```python
import functools

import jax
import jax.numpy as jnp
from jax import lax
from jax.experimental import pallas as pl
from jax.experimental.pallas import tpu as pltpu
from jax.sharding import PartitionSpec as P

D = 8192
HD = 128
NEW = 16
PAGE = 64
PATH_PAGES = 16
SHARED = 8
FAM = 4
RANKS = 16
PAIR = 15
ROOTS = 12
EXTRA = 3
NEAR = (0, 1, 3)
GROUPS = 2
LOG2E = 1.4426950408889634
MIB = 1024 * 1024


def split_kernel(pool_ref, fresh_ref, *refs):
    outs, sem = refs[:-1], refs[-1]
    pages_dev = pool_ref.shape[0]
    for i, out in enumerate(outs):
        lanes = pl.ds(i * HD, HD)
        pltpu.make_async_copy(pool_ref.at[:, :, lanes], out.at[pl.ds(0, pages_dev)], sem.at[i]).start()
        for p in range(EXTRA):
            rows = pl.ds(p * PAGE, PAGE)
            pltpu.make_async_copy(fresh_ref.at[rows, lanes], out.at[pages_dev + p], sem.at[i]).start()
    for i, out in enumerate(outs):
        pltpu.make_async_copy(out, out, sem.at[i]).wait()


def split(pool, fresh):
    hbm = pl.BlockSpec(memory_space=pltpu.HBM)
    vmem = pl.BlockSpec(memory_space=pltpu.VMEM)
    part = jax.ShapeDtypeStruct((pool.shape[0] + EXTRA, PAGE, HD), pool.dtype)
    return pl.pallas_call(
        split_kernel,
        out_shape=[part, part],
        in_specs=[hbm, hbm],
        out_specs=[vmem, vmem],
        scratch_shapes=[pltpu.SemaphoreType.DMA((2,))],
        compiler_params=pltpu.CompilerParams(vmem_limit_bytes=55 * MIB),
        name="split",
    )(pool, fresh)


def plan_kernel(pages_dev, rank_ref, table_ref, wanted_ref):
    rank = rank_ref[0]
    y, x = rank // 4, rank % 4
    slots, nodes = table_ref.shape
    table = table_ref[...]
    height = -(-pages_dev // 16) * 16
    per_rank = nodes // RANKS
    row = lax.broadcasted_iota(jnp.int32, (height, nodes), 0)
    node = lax.broadcasted_iota(jnp.int32, (nodes, 128), 0)
    column = lax.broadcasted_iota(jnp.int32, (nodes, 128), 1)
    step = column & 3
    begin = jnp.where(column < 16, ((y + step) & 3) * 4 + x, y * 4 + ((x + step) & 3)) * per_rank
    belongs = (node >= begin) & (node < begin + per_rank)
    low = lax.broadcasted_iota(jnp.int32, (height, height), 0)
    high = lax.broadcasted_iota(jnp.int32, (height, height), 1)
    earlier = (high < low).astype(jnp.bfloat16)
    page_id = lax.broadcasted_iota(jnp.int32, (height, 128), 0).astype(jnp.float32)
    line = lax.broadcasted_iota(jnp.int32, (16, 128), 0)
    wanted_ref[...] = jnp.zeros((16, 128), jnp.int32)

    @pl.loop(0, 8)
    def _(part):
        back = part % 4
        owner = jnp.where(part < 4, y * 4 + (x + 4 - back) % 4, (y + 4 - back) % 4 * 4 + x)
        base = owner * pages_dev
        hits = jnp.zeros((height, nodes), jnp.float32)
        for page in range(pages_dev):
            hit = jnp.max((table == base + page).astype(jnp.float32), axis=0, keepdims=True)
            hits = jnp.where(row == page, hit, hits)
        mine = (belongs & (column // 4 == part)).astype(jnp.bfloat16)
        present = jnp.dot(hits.astype(jnp.bfloat16), mine, preferred_element_type=jnp.float32) > 0
        before = jnp.dot(earlier, present.astype(jnp.bfloat16), preferred_element_type=jnp.float32)
        place = jnp.where(present, before, -1.0)
        wanted = jnp.zeros((16, 128), jnp.float32)
        for slot in range(PAIR):
            page = jnp.sum(jnp.where(place == slot, page_id, 0.0), axis=0, keepdims=True)
            wanted = jnp.where(line == slot, page, wanted)
        wanted_ref[...] += wanted.astype(jnp.int32)


def plan(rank, table, pages_dev):
    vmem = pl.BlockSpec(memory_space=pltpu.VMEM)
    return pl.pallas_call(
        functools.partial(plan_kernel, pages_dev),
        out_shape=jax.ShapeDtypeStruct((16, 128), jnp.int32),
        in_specs=[pl.BlockSpec(memory_space=pltpu.SMEM), vmem],
        out_specs=vmem,
        name="plan",
    )(rank, table)


def copy_pages(out, first, ref, wanted_ref, column, pages_dev):
    for slot in range(PAIR):
        page = jnp.clip(wanted_ref[slot, column], 0, pages_dev - 1)
        out[first + slot] = ref[page]


def pack_first_kernel(pages_dev, wanted_ref, *refs):
    sources, outs, (held, stage, in_sems, out_sem) = refs[:6], refs[6:14], refs[14:]
    near = len(NEAR)
    copies = [pltpu.make_async_copy(ref, held.at[k], in_sems.at[k]) for k, ref in enumerate(sources)]
    for copy in copies:
        copy.start()
    for i in range(2):
        for copy in copies[i * near : (i + 1) * near]:
            copy.wait()
        for e in (1, 3, 2, 0):
            part = stage.at[4 * i + e]
            for j, d in enumerate(NEAR):
                copy_pages(part, j * PAIR, held.at[i * near + j], wanted_ref, 16 * i + 4 * d + e, pages_dev)
            pltpu.make_async_copy(part, outs[4 * i + e], out_sem.at[4 * i + e]).start()
    for k, out in enumerate(outs):
        pltpu.make_async_copy(stage.at[k], out, out_sem.at[k]).wait()


def pack_first(wanted, pages_dev, keys, values):
    args = [keys[d] for d in NEAR] + [values[d] for d in NEAR]
    part = (len(NEAR) * PAIR, PAGE, HD)
    scratch = [pltpu.VMEM((len(args),) + keys[0].shape, jnp.bfloat16), pltpu.VMEM((8,) + part, jnp.bfloat16)]
    scratch += [pltpu.SemaphoreType.DMA((len(args),)), pltpu.SemaphoreType.DMA((8,))]
    return packing(functools.partial(pack_first_kernel, pages_dev), "pack_first", part, scratch, [wanted], args)


def packing(kernel, name, part, scratch, scalars, args):
    hbm = pl.BlockSpec(memory_space=pltpu.HBM)
    return pl.pallas_call(
        kernel,
        out_shape=[jax.ShapeDtypeStruct(part, jnp.bfloat16)] * 8,
        in_specs=[pl.BlockSpec(memory_space=pltpu.SMEM)] * len(scalars) + [hbm] * len(args),
        out_specs=[hbm] * 8,
        scratch_shapes=scratch,
        compiler_params=pltpu.CompilerParams(vmem_limit_bytes=62 * MIB),
        name=name,
    )(*scalars, *args)


def pack_second_kernel(pages_dev, rank_ref, parent_ref, wanted_ref, *refs):
    sources, outs, (far, roots, stage, in_sems, out_sem) = refs[:8], refs[8:16], refs[16:]
    y, x = rank_ref[0] // 4, rank_ref[0] % 4
    per_rank = parent_ref.shape[0] // RANKS
    copies = [
        pltpu.make_async_copy(ref.at[pl.ds(pages_dev, EXTRA)], roots.at[k], in_sems.at[k]) for k, ref in enumerate(sources)
    ]
    copies += [pltpu.make_async_copy(sources[4 * i + 2], far.at[i], in_sems.at[8 + i]) for i in range(2)]
    for copy in copies:
        copy.start()
    for copy in copies:
        copy.wait()
    for i in range(2):
        for e in (1, 3, 2, 0):
            part = stage.at[4 * i + e]
            copy_pages(part, 0, far.at[i], wanted_ref, 16 * i + 8 + e, pages_dev)
            dest = (y + e) % 4 * 4 + x if i == 0 else y * 4 + (x + e) % 4
            for child in range(per_rank - ROOTS):
                named = jnp.maximum(parent_ref[dest * per_rank + ROOTS + child], 0)
                up = named // per_rank
                away = (x + 4 - up % 4) % 4 if i == 0 else (y + 4 - up // 4) % 4
                root = jnp.minimum(named % per_rank, ROOTS - 1)
                rows = pl.ds(pl.multiple_of(root % 4 * NEW, NEW), NEW)
                part[PAIR + child // 4, child % 4 * NEW : (child % 4 + 1) * NEW, :] = roots[4 * i + away, root // 4, rows, :]
            pltpu.make_async_copy(part, outs[4 * i + e], out_sem.at[4 * i + e]).start()
    for k, out in enumerate(outs):
        pltpu.make_async_copy(stage.at[k], out, out_sem.at[k]).wait()


def pack_second(rank, parent, wanted, pages_dev, keys, values):
    part = (PAIR + EXTRA, PAGE, HD)
    scratch = [
        pltpu.VMEM((2,) + keys[0].shape, jnp.bfloat16),
        pltpu.VMEM((8, EXTRA, PAGE, HD), jnp.bfloat16),
        pltpu.VMEM((8,) + part, jnp.bfloat16),
        pltpu.SemaphoreType.DMA((10,)),
        pltpu.SemaphoreType.DMA((8,)),
    ]
    kernel = functools.partial(pack_second_kernel, pages_dev)
    return packing(kernel, "pack_second", part, scratch, [rank, parent, wanted], [*keys, *values])


def attend_family(first, node, at_refs, len_ref, above_refs, q_ref, fresh_ref, page_refs, attn_ref):
    scale = HD ** (-0.5) * LOG2E
    nt = (((1,), (1,)), ((), ()))

    def pages(i, n, slot):
        return [page_refs[i][at_refs[i][n * PATH_PAGES + slot + s]] for s in range(SHARED)]

    heads = q_ref.shape[1] // HD
    span = heads * NEW
    shared_key, shared_value = [jnp.concatenate(pages(i, node, 0), axis=0) for i in range(2)]
    queries = []
    for i in range(FAM):
        rows = q_ref[first + i * NEW : first + (i + 1) * NEW, :]
        queries.append(jnp.concatenate([rows[:, h * HD : (h + 1) * HD] for h in range(heads)], axis=0))
    s_shared = lax.dot_general(
        jnp.concatenate(queries, axis=0), shared_key, nt, preferred_element_type=jnp.float32
    )
    half = SHARED * PAGE // 2
    values, s_own = [], []
    for i in range(FAM):
        both = []
        for j in range(2):
            spot = jnp.maximum(above_refs[j][node + i], 0)
            upper = page_refs[j][spot // PAGE, pl.ds(pl.multiple_of(spot % PAGE, NEW), NEW), :]
            fresh = fresh_ref[first + i * NEW : first + (i + 1) * NEW, j * HD : (j + 1) * HD]
            both.append(jnp.concatenate(pages(j, node + i, SHARED) + [fresh, upper], axis=0))
        s = lax.dot_general(queries[i], both[0], nt, preferred_element_type=jnp.float32)
        late = s[:, half:]
        spot = lax.broadcasted_iota(jnp.int32, late.shape, 1) + SHARED * PAGE + half
        token = lax.broadcasted_iota(jnp.int32, late.shape, 0) % NEW
        key = spot - PATH_PAGES * PAGE
        limit = jnp.where(above_refs[0][node + i] >= 0, 2 * NEW, NEW)
        allowed = (spot < len_ref[node + i]) | ((key >= 0) & (key <= token)) | ((key >= NEW) & (key < limit))
        values.append(both[1])
        s_own.append(jnp.concatenate([s[:, :half], jnp.where(allowed, late, -jnp.inf)], axis=1))
    tops = [
        jnp.maximum(
            jnp.max(s_shared[i * span : (i + 1) * span], axis=1, keepdims=True),
            jnp.max(s_own[i], axis=1, keepdims=True),
        )
        for i in range(FAM)
    ]
    w_own = [jnp.exp2((s_own[i] - tops[i]) * scale).astype(jnp.bfloat16) for i in range(FAM)]
    w_shared = jnp.exp2((s_shared - jnp.concatenate(tops, axis=0)) * scale).astype(jnp.bfloat16)
    ones = jnp.ones((values[0].shape[0], HD), jnp.bfloat16)
    accum = [
        jnp.dot(w_own[i], jnp.concatenate([values[i], ones], axis=1), preferred_element_type=jnp.float32)
        for i in range(FAM)
    ]
    accum = jnp.concatenate(accum, axis=0) + jnp.dot(
        w_shared, jnp.concatenate([shared_value, ones[: SHARED * PAGE]], axis=1), preferred_element_type=jnp.float32
    )
    attn = (accum[:, :HD] / accum[:, HD:]).astype(jnp.bfloat16)
    for i in range(FAM):
        for h in range(heads):
            block = attn[i * span + h * NEW : i * span + (h + 1) * NEW, :]
            attn_ref[first + i * NEW : first + (i + 1) * NEW, h * HD : (h + 1) * HD] = block


def attend_kernel(*refs):
    at_refs, len_ref, above_refs, (q_ref, fresh_ref) = refs[:2], refs[2], refs[3:5], refs[5:7]
    sources, w_hbm, (attn_ref, w_ref), page_refs, sems = (refs[7:15], refs[15:23]), refs[23], refs[24:26], refs[26:28], refs[28]
    for i in range(2):
        start = 0
        for ref in sources[i]:
            count = ref.shape[0]
            pltpu.make_async_copy(ref, page_refs[i].at[pl.ds(start, count)], sems.at[i]).start()
            start += count
    weights = []
    for part in range(8):
        rows = pl.ds(part * (w_ref.shape[0] // 8), w_ref.shape[0] // 8)
        weights.append(pltpu.make_async_copy(w_hbm.at[rows], w_ref.at[rows], sems.at[2 + part]))
        weights[-1].start()
    for i in range(2):
        pltpu.make_async_copy(page_refs[i], page_refs[i], sems.at[i]).wait()
    for f in range(q_ref.shape[0] // (FAM * NEW)):
        attend_family(f * FAM * NEW, f * FAM, at_refs, len_ref, above_refs, q_ref, fresh_ref, page_refs, attn_ref)
    for copy in weights:
        copy.wait()


def attend(at, lengths, above, queries, fresh, keys, values, w_out):
    rows, width = queries.shape
    smem = pl.BlockSpec(memory_space=pltpu.SMEM)
    vmem = pl.BlockSpec(memory_space=pltpu.VMEM)
    hbm = pl.BlockSpec(memory_space=pltpu.HBM)
    pages = pltpu.VMEM((sum(k.shape[0] for k in keys), PAGE, HD), jnp.bfloat16)
    return pl.pallas_call(
        attend_kernel,
        out_shape=[pltpu.VMEM((rows, width), jnp.bfloat16), pltpu.VMEM(w_out.shape, w_out.dtype)],
        in_specs=[smem] * 5 + [vmem] * 2 + [hbm] * 17,
        out_specs=[vmem, vmem],
        scratch_shapes=[pages, pages, pltpu.SemaphoreType.DMA((10,))],
        compiler_params=pltpu.CompilerParams(vmem_limit_bytes=44 * MIB),
        cost_estimate=pl.CostEstimate(
            flops=4 * rows * width * 1056 * 4, bytes_accessed=4 * rows * width, transcendentals=rows * 8 * 1056
        ),
        name="attend",
    )(*at, lengths, *above, queries, fresh, *keys, *values, w_out)


def project_kernel(order_ref, attn_ref, w_ref, out_ref):
    count, rows, cols = out_ref.shape

    @pl.loop(0, count)
    def _(b):
        w = w_ref[:, pl.ds(pl.multiple_of(order_ref[b] * cols, cols), cols)]
        out_ref[b] = jnp.dot(attn_ref[...], w, preferred_element_type=jnp.float32).astype(jnp.bfloat16)


def project(order, attn, w_out):
    rows, depth = attn.shape
    cols = w_out.shape[1] // 8
    count = order.shape[0]
    smem = pl.BlockSpec(memory_space=pltpu.SMEM)
    vmem = pl.BlockSpec(memory_space=pltpu.VMEM)
    return pl.pallas_call(
        project_kernel,
        out_shape=jax.ShapeDtypeStruct((count, rows, cols), jnp.bfloat16),
        in_specs=[smem, vmem, vmem],
        out_specs=vmem,
        compiler_params=pltpu.CompilerParams(vmem_limit_bytes=12 * MIB),
        cost_estimate=pl.CostEstimate(
            flops=2 * rows * depth * cols * count, bytes_accessed=rows * cols * count * 2, transcendentals=0
        ),
        name="project",
    )(order, attn, w_out)


def shift(dy, dx):
    return [(s, (s // 4 + dy) % 4 * 4 + (s % 4 + dx) % 4) for s in range(RANKS)]


def turn(d):
    return [(t, (t + 2 * d) % 8) for t in range(8)]


def places_of(table, path_parent, rank, pages_dev, nodes):
    owner = table // pages_dev
    other, mine = table[None, :], table[:, None]
    slot = jnp.arange(table.shape[0], dtype=jnp.int32)
    first = (slot % PATH_PAGES >= SHARED) | (slot // PATH_PAGES % FAM == 0)
    before = (other < mine) & (other >= (owner * pages_dev)[:, None]) & first[None, :]
    place = jnp.sum(before.astype(jnp.int32), axis=1)
    child = jnp.arange(nodes, dtype=jnp.int32) - ROOTS
    up = jnp.maximum(path_parent, 0) // nodes
    many, few = len(NEAR) * PAIR, PAIR + EXTRA

    def turns(r):
        return (rank // 4 - r // 4) % 4, (rank % 4 - r % 4) % 4

    at, above = [], []
    for i in range(2):
        e, d = turns(owner)[:: 1 - 2 * i]
        at.append(jnp.where(d == 2, 4 * many + e * few, e * many + jnp.minimum(d, 2) * PAIR) + place)
        row = (4 * many + turns(up)[i] * few + PAIR) * PAGE + child * NEW
        above.append(jnp.where((path_parent >= 0) & (child >= 0), row, -1))
    return at, above


def far_kernel(kept_ref, back_ref, *out_refs):
    rows = out_refs[0].shape[0]
    for i, ref in enumerate(out_refs):
        part = pl.ds(i * rows, rows)
        ref[...] = (kept_ref[1, part].astype(jnp.float32) + back_ref[part].astype(jnp.float32)).astype(jnp.bfloat16)


def near_kernel(first, kept_ref, back_ref, from_low_ref, from_high_ref, up_ref, down_ref):
    half = from_low_ref.shape[0]
    low, high = pl.ds(0, half), pl.ds(half, half)

    def pair(i, start):
        part = pl.ds(first + start, half)
        return kept_ref[i, part].astype(jnp.float32) + back_ref[i, part].astype(jnp.float32)

    up_ref[low] = (pair(0, 0) + from_low_ref[...].astype(jnp.float32)).astype(jnp.bfloat16)
    up_ref[high] = pair(0, half).astype(jnp.bfloat16)
    down_ref[low] = pair(1, 0).astype(jnp.bfloat16)
    down_ref[high] = (pair(1, half) + from_high_ref[...].astype(jnp.float32)).astype(jnp.bfloat16)


def last_kernel(first, kept_ref, back_ref, up_ref, down_ref, residual_ref, mixed_ref, power_ref):
    part = pl.ds(first, up_ref.shape[0])
    mixed = residual_ref[part].astype(jnp.float32)
    for term in (kept_ref[2, part], back_ref[2, part], up_ref[...], down_ref[...]):
        mixed = mixed + term.astype(jnp.float32)
    mixed_ref[...] = mixed
    power_ref[...] = lax.dot_general(
        jnp.ones((8, mixed.shape[1]), jnp.float32),
        mixed * mixed,
        (((1,), (1,)), ((), ())),
        precision=lax.Precision.HIGHEST,
        preferred_element_type=jnp.float32,
    )


def local(kernel, name, outs, *args, scalars=0, limit=12):
    vmem = pl.BlockSpec(memory_space=pltpu.VMEM)
    smem = pl.BlockSpec(memory_space=pltpu.SMEM)
    return pl.pallas_call(
        kernel,
        out_shape=[jax.ShapeDtypeStruct(shape, dtype) for shape, dtype in outs],
        in_specs=[smem] * scalars + [vmem] * (len(args) - scalars),
        out_specs=[vmem] * len(outs),
        compiler_params=pltpu.CompilerParams(vmem_limit_bytes=limit * MIB),
        name=name,
    )(*args)


def body(queries, fresh_kv, kv_pool, page_table, path_len, parent, w_out, residual, gain):
    rank = lax.axis_index("dp")
    tensor_rank = lax.axis_index("tensor")
    tensors = lax.axis_size("tensor")
    rows = queries.shape[0]
    nodes = rows // NEW
    pages_dev = kv_pool.shape[0]
    key, value = split(kv_pool, fresh_kv)
    place = rank.reshape(1)
    wanted = plan(place, page_table.T, pages_dev)
    far_key, far_value, wanted = lax.optimization_barrier((key, value, wanted))
    keys = [key] + [lax.ppermute(far_key if d == 2 else key, "dp", shift(0, d)) for d in (1, 2, 3)]
    values = [value] + [lax.ppermute(far_value if d == 2 else value, "dp", shift(d, 0)) for d in (1, 2, 3)]
    first = list(pack_first(wanted, pages_dev, keys, values))

    def deliver(parts):
        order = [(e, i) for e in (1, 3, 2) for i in range(2)]
        return {(i, e): lax.ppermute(parts[4 * i + e], "dp", shift(0, e) if i else shift(e, 0)) for e, i in order}

    got = deliver(first)
    got[0, 1], wanted = lax.optimization_barrier((got[0, 1], wanted))
    second = list(pack_second(place, parent, wanted, pages_dev, keys, values))
    for i, e in got:
        if (i, e) != (0, 1):
            got[i, e], second[4 * i + e] = lax.optimization_barrier((got[i, e], second[4 * i + e]))
    more = deliver(second)
    keys, values = (
        [first[4 * i]] + [got[i, e] for e in (1, 2, 3)] + [second[4 * i]] + [more[i, e] for e in (1, 2, 3)]
        for i in range(2)
    )
    keys, values, w_out, residual, gain = lax.optimization_barrier((keys, values, w_out, residual, gain))

    own_table = lax.dynamic_slice_in_dim(page_table, rank * nodes, nodes).reshape(-1)
    lengths = lax.dynamic_slice_in_dim(path_len, rank * nodes, nodes)
    at, above = places_of(own_table, lax.dynamic_slice_in_dim(parent, rank * nodes, nodes), rank, pages_dev, nodes)
    z, core = tensor_rank // 2, tensor_rank % 2
    far, rest = (z + 2) % 4 * 2, (z + jnp.array([1, 3, 0], jnp.int32)) % 4 * 2
    far = jnp.stack([far + 1 - core, far + core])
    other, same = rest + 1 - core, rest + core

    attn, w_held = attend(at, lengths, above, queries, fresh_kv, keys, values, w_out)

    swap = [(t, t ^ 1) for t in range(tensors)]
    cols = D // tensors
    mine = lax.dynamic_slice_in_dim(residual, tensor_rank * cols, cols, 1)
    group = rows // GROUPS
    both = project(far, attn, w_held)
    both, attn = lax.optimization_barrier((both, attn))
    far_back = lax.ppermute(both[0], "tensor", swap)
    away = project(other, attn, w_held)
    far_back, away, attn = lax.optimization_barrier((far_back, away, attn))
    back = lax.ppermute(away, "tensor", swap)
    halves = [((group // 2, cols), jnp.bfloat16)] * (2 * GROUPS)
    sent = local(far_kernel, "far", halves, both, far_back)
    *sent, attn = lax.optimization_barrier((*sent, attn))
    low = [lax.ppermute(sent[2 * g], "tensor", turn(1)) for g in range(GROUPS)]
    high = [lax.ppermute(sent[2 * g + 1], "tensor", turn(-1)) for g in range(GROUPS)]
    kept = project(same, attn, w_held)
    whole = ((group, cols), jnp.bfloat16)
    ups, downs = [], []
    for g in range(GROUPS):
        up, down = local(
            functools.partial(near_kernel, g * group), "near", [whole, whole], kept, back, low[g], high[g]
        )
        ups.append(lax.ppermute(up, "tensor", turn(1)))
        downs.append(lax.ppermute(down, "tensor", turn(-1)))
    outs = [((group, cols), jnp.float32), ((8, group), jnp.float32)]
    done = [
        local(functools.partial(last_kernel, g * group), "last", outs, kept, back, ups[g], downs[g], mine)
        for g in range(GROUPS)
    ]

    mixed = jnp.concatenate([m for m, _ in done], axis=0)
    power = jnp.concatenate([p for _, p in done], axis=1)
    power = power + lax.ppermute(power, "tensor", swap)
    total = power
    for d in (1, 2, 3):
        total = total + lax.ppermute(power, "tensor", turn(d))
    norm = lax.rsqrt(total[0].reshape(rows, 1) / D + 1e-05)
    own_gain = lax.dynamic_slice_in_dim(gain, tensor_rank * cols, cols)
    normed = mixed * norm * own_gain.astype(jnp.float32)
    return (mixed.astype(jnp.bfloat16), normed.astype(jnp.bfloat16))


def solution(mesh):
    return jax.shard_map(
        body,
        mesh=mesh,
        in_specs=(
            P("dp", "tensor"),
            P("dp", "tensor"),
            P("dp", None, "tensor"),
            P(),
            P(),
            P(),
            P("tensor", None),
            P("dp", None),
            P(),
        ),
        out_specs=(P("dp", "tensor"), P("dp", "tensor")),
        check_vma=False,
    )
```

```python
import functools

import jax
import jax.numpy as jnp
from jax import lax
from jax.experimental import pallas as pl
from jax.experimental.pallas import tpu as pltpu
from jax.sharding import PartitionSpec as P

D = 8192
HD = 128
NEW = 16
PAGE = 64
PATH_PAGES = 16
SHARED = 8
FAM = 4
RANKS = 16
PAIR = 15
ROOTS = 12
EXTRA = 3
CHUNK = 6
NEAR = (0, 1, 3)
GROUPS = 2
LOG2E = 1.4426950408889634
MIB = 1024 * 1024


def split_kernel(pool_ref, fresh_ref, *refs):
    outs, sem = refs[:-1], refs[-1]
    pages_dev = pool_ref.shape[0]
    for i, out in enumerate(outs):
        lanes = pl.ds(i * HD, HD)
        for start in range(0, pages_dev, CHUNK):
            some = pl.ds(start, min(CHUNK, pages_dev - start))
            pltpu.make_async_copy(pool_ref.at[some, :, lanes], out.at[some], sem.at[i]).start()
        for p in range(EXTRA):
            rows = pl.ds(p * PAGE, PAGE)
            pltpu.make_async_copy(fresh_ref.at[rows, lanes], out.at[pages_dev + p], sem.at[i]).start()
    for i, out in enumerate(outs):
        pltpu.make_async_copy(out, out, sem.at[i]).wait()


def split(pool, fresh):
    hbm = pl.BlockSpec(memory_space=pltpu.HBM)
    vmem = pl.BlockSpec(memory_space=pltpu.VMEM)
    part = pltpu.VMEM((pool.shape[0] + EXTRA, PAGE, HD), pool.dtype)
    return pl.pallas_call(
        split_kernel,
        out_shape=[part, part],
        in_specs=[hbm, hbm],
        out_specs=[vmem, vmem],
        scratch_shapes=[pltpu.SemaphoreType.DMA((2,))],
        compiler_params=pltpu.CompilerParams(vmem_limit_bytes=61 * MIB),
        name="split",
    )(pool, fresh)


def plan_kernel(pages_dev, rank_ref, table_ref, wanted_ref):
    rank = rank_ref[0]
    y, x = rank // 4, rank % 4
    slots, nodes = table_ref.shape
    table = table_ref[...]
    height = -(-pages_dev // 16) * 16
    per_rank = nodes // RANKS
    row = lax.broadcasted_iota(jnp.int32, (height, nodes), 0)
    node = lax.broadcasted_iota(jnp.int32, (nodes, 128), 0)
    column = lax.broadcasted_iota(jnp.int32, (nodes, 128), 1)
    step = column & 3
    begin = jnp.where(column < 16, ((y + step) & 3) * 4 + x, y * 4 + ((x + step) & 3)) * per_rank
    belongs = (node >= begin) & (node < begin + per_rank)
    low = lax.broadcasted_iota(jnp.int32, (height, height), 0)
    high = lax.broadcasted_iota(jnp.int32, (height, height), 1)
    earlier = (high < low).astype(jnp.bfloat16)
    page_id = lax.broadcasted_iota(jnp.int32, (height, 128), 0).astype(jnp.float32)
    line = lax.broadcasted_iota(jnp.int32, (16, 128), 0)
    wanted_ref[...] = jnp.zeros((16, 128), jnp.int32)

    @pl.loop(0, 8)
    def _(part):
        back = part % 4
        owner = jnp.where(part < 4, y * 4 + (x + 4 - back) % 4, (y + 4 - back) % 4 * 4 + x)
        base = owner * pages_dev
        hits = jnp.zeros((height, nodes), jnp.float32)
        for page in range(pages_dev):
            hit = jnp.max((table == base + page).astype(jnp.float32), axis=0, keepdims=True)
            hits = jnp.where(row == page, hit, hits)
        mine = (belongs & (column // 4 == part)).astype(jnp.bfloat16)
        present = jnp.dot(hits.astype(jnp.bfloat16), mine, preferred_element_type=jnp.float32) > 0
        before = jnp.dot(earlier, present.astype(jnp.bfloat16), preferred_element_type=jnp.float32)
        place = jnp.where(present, before, -1.0)
        wanted = jnp.zeros((16, 128), jnp.float32)
        for slot in range(PAIR):
            page = jnp.sum(jnp.where(place == slot, page_id, 0.0), axis=0, keepdims=True)
            wanted = jnp.where(line == slot, page, wanted)
        wanted_ref[...] += wanted.astype(jnp.int32)


def plan(rank, table, pages_dev):
    vmem = pl.BlockSpec(memory_space=pltpu.VMEM)
    return pl.pallas_call(
        functools.partial(plan_kernel, pages_dev),
        out_shape=jax.ShapeDtypeStruct((16, 128), jnp.int32),
        in_specs=[pl.BlockSpec(memory_space=pltpu.SMEM), vmem],
        out_specs=vmem,
        name="plan",
    )(rank, table)


def copy_pages(out, first, ref, wanted_ref, column, pages_dev):
    for slot in range(PAIR):
        page = jnp.clip(wanted_ref[slot, column], 0, pages_dev - 1)
        out[first + slot] = ref[page]


def pack_first_kernel(pages_dev, wanted_ref, *refs):
    sources, outs, (held, stage, in_sems, out_sem) = refs[:6], refs[6:14], refs[14:]
    near = len(NEAR)
    copies = [pltpu.make_async_copy(ref, held.at[k], in_sems.at[k]) for k, ref in enumerate(sources)]
    for copy in copies:
        copy.start()
    for i in range(2):
        for copy in copies[i * near : (i + 1) * near]:
            copy.wait()
        for e in (1, 3, 2, 0):
            part = stage.at[4 * i + e]
            for j, d in enumerate(NEAR):
                copy_pages(part, j * PAIR, held.at[i * near + j], wanted_ref, 16 * i + 4 * d + e, pages_dev)
            pltpu.make_async_copy(part, outs[4 * i + e], out_sem.at[4 * i + e]).start()
    for k, out in enumerate(outs):
        pltpu.make_async_copy(stage.at[k], out, out_sem.at[k]).wait()


def pack_first(wanted, pages_dev, keys, values):
    args = [keys[d] for d in NEAR] + [values[d] for d in NEAR]
    part = (len(NEAR) * PAIR, PAGE, HD)
    scratch = [pltpu.VMEM((len(args),) + keys[0].shape, jnp.bfloat16), pltpu.VMEM((8,) + part, jnp.bfloat16)]
    scratch += [pltpu.SemaphoreType.DMA((len(args),)), pltpu.SemaphoreType.DMA((8,))]
    return packing(functools.partial(pack_first_kernel, pages_dev), "pack_first", part, scratch, [wanted], args)


def packing(kernel, name, part, scratch, scalars, args):
    hbm = pl.BlockSpec(memory_space=pltpu.HBM)
    return pl.pallas_call(
        kernel,
        out_shape=[jax.ShapeDtypeStruct(part, jnp.bfloat16)] * 8,
        in_specs=[pl.BlockSpec(memory_space=pltpu.SMEM)] * len(scalars) + [hbm] * len(args),
        out_specs=[hbm] * 8,
        scratch_shapes=scratch,
        compiler_params=pltpu.CompilerParams(vmem_limit_bytes=62 * MIB),
        name=name,
    )(*scalars, *args)


def pack_second_kernel(pages_dev, rank_ref, parent_ref, wanted_ref, *refs):
    sources, outs, (far, roots, stage, in_sems, out_sem) = refs[:8], refs[8:16], refs[16:]
    y, x = rank_ref[0] // 4, rank_ref[0] % 4
    per_rank = parent_ref.shape[0] // RANKS
    copies = [
        pltpu.make_async_copy(ref.at[pl.ds(pages_dev, EXTRA)], roots.at[k], in_sems.at[k]) for k, ref in enumerate(sources)
    ]
    copies += [pltpu.make_async_copy(sources[4 * i + 2], far.at[i], in_sems.at[8 + i]) for i in range(2)]
    for copy in copies:
        copy.start()
    for copy in copies:
        copy.wait()
    for i in range(2):
        for e in (1, 3, 2, 0):
            part = stage.at[4 * i + e]
            copy_pages(part, 0, far.at[i], wanted_ref, 16 * i + 8 + e, pages_dev)
            dest = (y + e) % 4 * 4 + x if i == 0 else y * 4 + (x + e) % 4
            for child in range(per_rank - ROOTS):
                named = jnp.maximum(parent_ref[dest * per_rank + ROOTS + child], 0)
                up = named // per_rank
                away = (x + 4 - up % 4) % 4 if i == 0 else (y + 4 - up // 4) % 4
                root = jnp.minimum(named % per_rank, ROOTS - 1)
                rows = pl.ds(pl.multiple_of(root % 4 * NEW, NEW), NEW)
                part[PAIR + child // 4, child % 4 * NEW : (child % 4 + 1) * NEW, :] = roots[4 * i + away, root // 4, rows, :]
            pltpu.make_async_copy(part, outs[4 * i + e], out_sem.at[4 * i + e]).start()
    for k, out in enumerate(outs):
        pltpu.make_async_copy(stage.at[k], out, out_sem.at[k]).wait()


def pack_second(rank, parent, wanted, pages_dev, keys, values):
    part = (PAIR + EXTRA, PAGE, HD)
    scratch = [
        pltpu.VMEM((2,) + keys[0].shape, jnp.bfloat16),
        pltpu.VMEM((8, EXTRA, PAGE, HD), jnp.bfloat16),
        pltpu.VMEM((8,) + part, jnp.bfloat16),
        pltpu.SemaphoreType.DMA((10,)),
        pltpu.SemaphoreType.DMA((8,)),
    ]
    kernel = functools.partial(pack_second_kernel, pages_dev)
    return packing(kernel, "pack_second", part, scratch, [rank, parent, wanted], [*keys, *values])


def attend_family(wait_values, first, node, at_refs, len_ref, above_refs, q_ref, fresh_ref, page_refs, attn_ref):
    scale = HD ** (-0.5) * LOG2E
    nt = (((1,), (1,)), ((), ()))

    def pages(i, n, slot):
        return [page_refs[i][at_refs[i][n * PATH_PAGES + slot + s]] for s in range(SHARED)]

    heads = q_ref.shape[1] // HD
    span = heads * NEW
    shared_key = jnp.concatenate(pages(0, node, 0), axis=0)
    queries = []
    for i in range(FAM):
        rows = q_ref[first + i * NEW : first + (i + 1) * NEW, :]
        queries.append(jnp.concatenate([rows[:, h * HD : (h + 1) * HD] for h in range(heads)], axis=0))
    s_shared = lax.dot_general(
        jnp.concatenate(queries, axis=0), shared_key, nt, preferred_element_type=jnp.float32
    )
    half = SHARED * PAGE // 2
    def near(j, i):
        spot = jnp.maximum(above_refs[j][node + i], 0)
        upper = page_refs[j][spot // PAGE, pl.ds(pl.multiple_of(spot % PAGE, NEW), NEW), :]
        fresh = fresh_ref[first + i * NEW : first + (i + 1) * NEW, j * HD : (j + 1) * HD]
        return jnp.concatenate(pages(j, node + i, SHARED) + [fresh, upper], axis=0)

    s_own = []
    for i in range(FAM):
        s = lax.dot_general(queries[i], near(0, i), nt, preferred_element_type=jnp.float32)
        late = s[:, half:]
        spot = lax.broadcasted_iota(jnp.int32, late.shape, 1) + SHARED * PAGE + half
        token = lax.broadcasted_iota(jnp.int32, late.shape, 0) % NEW
        key = spot - PATH_PAGES * PAGE
        limit = jnp.where(above_refs[0][node + i] >= 0, 2 * NEW, NEW)
        allowed = (spot < len_ref[node + i]) | ((key >= 0) & (key <= token)) | ((key >= NEW) & (key < limit))
        s_own.append(jnp.concatenate([s[:, :half], jnp.where(allowed, late, -jnp.inf)], axis=1))
    tops = [
        jnp.maximum(
            jnp.max(s_shared[i * span : (i + 1) * span], axis=1, keepdims=True),
            jnp.max(s_own[i], axis=1, keepdims=True),
        )
        for i in range(FAM)
    ]
    w_own = [jnp.exp2((s_own[i] - tops[i]) * scale).astype(jnp.bfloat16) for i in range(FAM)]
    w_shared = jnp.exp2((s_shared - jnp.concatenate(tops, axis=0)) * scale).astype(jnp.bfloat16)
    wait_values()
    values = [near(1, i) for i in range(FAM)]
    shared_value = jnp.concatenate(pages(1, node, 0), axis=0)
    ones = jnp.ones((values[0].shape[0], HD), jnp.bfloat16)
    accum = [
        jnp.dot(w_own[i], jnp.concatenate([values[i], ones], axis=1), preferred_element_type=jnp.float32)
        for i in range(FAM)
    ]
    accum = jnp.concatenate(accum, axis=0) + jnp.dot(
        w_shared, jnp.concatenate([shared_value, ones[: SHARED * PAGE]], axis=1), preferred_element_type=jnp.float32
    )
    attn = (accum[:, :HD] / accum[:, HD:]).astype(jnp.bfloat16)
    for i in range(FAM):
        for h in range(heads):
            block = attn[i * span + h * NEW : i * span + (h + 1) * NEW, :]
            attn_ref[first + i * NEW : first + (i + 1) * NEW, h * HD : (h + 1) * HD] = block


def attend_kernel(*refs):
    at_refs, len_ref, above_refs, (q_ref, fresh_ref) = refs[:2], refs[2], refs[3:5], refs[5:7]
    sources, w_hbm, (attn_ref, w_ref), page_refs, sems = (refs[7:15], refs[15:23]), refs[23], refs[24:26], refs[26:28], refs[28]
    for i in range(2):
        start = 0
        for ref in sources[i]:
            count = ref.shape[0]
            pltpu.make_async_copy(ref, page_refs[i].at[pl.ds(start, count)], sems.at[i]).start()
            start += count
    weights = []
    for part in range(8):
        rows = pl.ds(part * (w_ref.shape[0] // 8), w_ref.shape[0] // 8)
        weights.append(pltpu.make_async_copy(w_hbm.at[rows], w_ref.at[rows], sems.at[2 + part]))
        weights[-1].start()
    all_pages = [pltpu.make_async_copy(page_refs[i], page_refs[i], sems.at[i]) for i in range(2)]
    all_pages[0].wait()
    for f in range(q_ref.shape[0] // (FAM * NEW)):
        wait_values = all_pages[1].wait if f == 0 else lambda: None
        attend_family(
            wait_values, f * FAM * NEW, f * FAM, at_refs, len_ref, above_refs, q_ref, fresh_ref, page_refs, attn_ref
        )
    for copy in weights:
        copy.wait()


def attend(at, lengths, above, queries, fresh, keys, values, w_out):
    rows, width = queries.shape
    smem = pl.BlockSpec(memory_space=pltpu.SMEM)
    vmem = pl.BlockSpec(memory_space=pltpu.VMEM)
    hbm = pl.BlockSpec(memory_space=pltpu.HBM)
    pages = pltpu.VMEM((sum(k.shape[0] for k in keys), PAGE, HD), jnp.bfloat16)
    return pl.pallas_call(
        attend_kernel,
        out_shape=[pltpu.VMEM((rows, width), jnp.bfloat16), pltpu.VMEM(w_out.shape, w_out.dtype)],
        in_specs=[smem] * 5 + [vmem] * 2 + [hbm] * 17,
        out_specs=[vmem, vmem],
        scratch_shapes=[pages, pages, pltpu.SemaphoreType.DMA((10,))],
        compiler_params=pltpu.CompilerParams(vmem_limit_bytes=44 * MIB),
        cost_estimate=pl.CostEstimate(
            flops=4 * rows * width * 1056 * 4, bytes_accessed=4 * rows * width, transcendentals=rows * 8 * 1056
        ),
        name="attend",
    )(*at, lengths, *above, queries, fresh, *keys, *values, w_out)


def project_kernel(order_ref, attn_ref, w_ref, out_ref):
    count, rows, cols = out_ref.shape

    @pl.loop(0, count)
    def _(b):
        w = w_ref[:, pl.ds(pl.multiple_of(order_ref[b] * cols, cols), cols)]
        out_ref[b] = jnp.dot(attn_ref[...], w, preferred_element_type=jnp.float32).astype(jnp.bfloat16)


def project(order, attn, w_out):
    rows, depth = attn.shape
    cols = w_out.shape[1] // 8
    count = order.shape[0]
    smem = pl.BlockSpec(memory_space=pltpu.SMEM)
    vmem = pl.BlockSpec(memory_space=pltpu.VMEM)
    return pl.pallas_call(
        project_kernel,
        out_shape=jax.ShapeDtypeStruct((count, rows, cols), jnp.bfloat16),
        in_specs=[smem, vmem, vmem],
        out_specs=vmem,
        compiler_params=pltpu.CompilerParams(vmem_limit_bytes=12 * MIB),
        cost_estimate=pl.CostEstimate(
            flops=2 * rows * depth * cols * count, bytes_accessed=rows * cols * count * 2, transcendentals=0
        ),
        name="project",
    )(order, attn, w_out)


def shift(dy, dx):
    return [(s, (s // 4 + dy) % 4 * 4 + (s % 4 + dx) % 4) for s in range(RANKS)]


def turn(d):
    return [(t, (t + 2 * d) % 8) for t in range(8)]


def places_of(table, path_parent, rank, pages_dev, nodes):
    owner = table // pages_dev
    other, mine = table[None, :], table[:, None]
    slot = jnp.arange(table.shape[0], dtype=jnp.int32)
    first = (slot % PATH_PAGES >= SHARED) | (slot // PATH_PAGES % FAM == 0)
    before = (other < mine) & (other >= (owner * pages_dev)[:, None]) & first[None, :]
    place = jnp.sum(before.astype(jnp.int32), axis=1)
    child = jnp.arange(nodes, dtype=jnp.int32) - ROOTS
    up = jnp.maximum(path_parent, 0) // nodes
    many, few = len(NEAR) * PAIR, PAIR + EXTRA

    def turns(r):
        return (rank // 4 - r // 4) % 4, (rank % 4 - r % 4) % 4

    at, above = [], []
    for i in range(2):
        e, d = turns(owner)[:: 1 - 2 * i]
        at.append(jnp.where(d == 2, 4 * many + e * few, e * many + jnp.minimum(d, 2) * PAIR) + place)
        row = (4 * many + turns(up)[i] * few + PAIR) * PAGE + child * NEW
        above.append(jnp.where((path_parent >= 0) & (child >= 0), row, -1))
    return at, above


def far_kernel(kept_ref, back_ref, *out_refs):
    rows = out_refs[0].shape[0]
    for i, ref in enumerate(out_refs):
        part = pl.ds(i * rows, rows)
        ref[...] = (kept_ref[1, part].astype(jnp.float32) + back_ref[part].astype(jnp.float32)).astype(jnp.bfloat16)


def near_kernel(first, kept_ref, back_ref, from_low_ref, from_high_ref, up_ref, down_ref):
    half = from_low_ref.shape[0]
    low, high = pl.ds(0, half), pl.ds(half, half)

    def pair(i, start):
        part = pl.ds(first + start, half)
        return kept_ref[i, part].astype(jnp.float32) + back_ref[i, part].astype(jnp.float32)

    up_ref[low] = (pair(0, 0) + from_low_ref[...].astype(jnp.float32)).astype(jnp.bfloat16)
    up_ref[high] = pair(0, half).astype(jnp.bfloat16)
    down_ref[low] = pair(1, 0).astype(jnp.bfloat16)
    down_ref[high] = (pair(1, half) + from_high_ref[...].astype(jnp.float32)).astype(jnp.bfloat16)


def last_kernel(kept_ref, back_ref, up_ref, down_ref, residual_ref, mixed_ref, power_ref):
    mixed = residual_ref[...].astype(jnp.float32)
    for term in (kept_ref[0], back_ref[0], up_ref[...], down_ref[...]):
        mixed = mixed + term.astype(jnp.float32)
    mixed_ref[...] = mixed
    squares = mixed * mixed
    power_ref[...] = lax.dot_general(
        jnp.ones((8, 128), jnp.float32),
        sum(squares[:, start : start + 128] for start in range(0, mixed.shape[1], 128)),
        (((1,), (1,)), ((), ())),
        precision=lax.Precision.HIGHEST,
        preferred_element_type=jnp.float32,
    )


def last(g, kept, back, up, down, residual):
    group, cols = up.shape
    own = pl.BlockSpec((1, group, cols), lambda i: (2, g, 0))
    whole = pl.BlockSpec((group, cols), lambda i: (0, 0))
    return pl.pallas_call(
        last_kernel,
        out_shape=[jax.ShapeDtypeStruct((group, cols), jnp.float32), jax.ShapeDtypeStruct((8, group), jnp.float32)],
        grid=(1,),
        in_specs=[own, own, whole, whole, pl.BlockSpec((group, cols), lambda i: (g, 0))],
        out_specs=[whole, pl.BlockSpec((8, group), lambda i: (0, 0))],
        compiler_params=pltpu.CompilerParams(vmem_limit_bytes=12 * MIB),
        name="last",
    )(kept, back, up, down, residual)


def local(kernel, name, outs, *args, scalars=0, limit=12):
    vmem = pl.BlockSpec(memory_space=pltpu.VMEM)
    smem = pl.BlockSpec(memory_space=pltpu.SMEM)
    return pl.pallas_call(
        kernel,
        out_shape=[jax.ShapeDtypeStruct(*out) if isinstance(out, tuple) else out for out in outs],
        in_specs=[smem] * scalars + [vmem] * (len(args) - scalars),
        out_specs=[vmem] * len(outs),
        compiler_params=pltpu.CompilerParams(vmem_limit_bytes=limit * MIB),
        name=name,
    )(*args)


def body(queries, fresh_kv, kv_pool, page_table, path_len, parent, w_out, residual, gain):
    rank = lax.axis_index("dp")
    tensor_rank = lax.axis_index("tensor")
    tensors = lax.axis_size("tensor")
    rows = queries.shape[0]
    nodes = rows // NEW
    pages_dev = kv_pool.shape[0]
    key, value = split(kv_pool, fresh_kv)
    place = rank.reshape(1)
    wanted = plan(place, page_table.T, pages_dev)
    far_key, far_value, wanted = lax.optimization_barrier((key, value, wanted))
    keys = [key] + [lax.ppermute(far_key if d == 2 else key, "dp", shift(0, d)) for d in (1, 2, 3)]
    values = [value] + [lax.ppermute(far_value if d == 2 else value, "dp", shift(d, 0)) for d in (1, 2, 3)]
    first = list(pack_first(wanted, pages_dev, keys, values))

    def deliver(parts):
        order = [(e, i) for e in (1, 3, 2) for i in range(2)]
        return {(i, e): lax.ppermute(parts[4 * i + e], "dp", shift(0, e) if i else shift(e, 0)) for e, i in order}

    got = deliver(first)
    got[0, 1], wanted = lax.optimization_barrier((got[0, 1], wanted))
    second = list(pack_second(place, parent, wanted, pages_dev, keys, values))
    for i, e in got:
        if (i, e) != (0, 1):
            got[i, e], second[4 * i + e] = lax.optimization_barrier((got[i, e], second[4 * i + e]))
    more = deliver(second)
    keys, values = (
        [first[4 * i]] + [got[i, e] for e in (1, 2, 3)] + [second[4 * i]] + [more[i, e] for e in (1, 2, 3)]
        for i in range(2)
    )
    keys, values, w_out, residual, gain = lax.optimization_barrier((keys, values, w_out, residual, gain))

    own_table = lax.dynamic_slice_in_dim(page_table, rank * nodes, nodes).reshape(-1)
    lengths = lax.dynamic_slice_in_dim(path_len, rank * nodes, nodes)
    at, above = places_of(own_table, lax.dynamic_slice_in_dim(parent, rank * nodes, nodes), rank, pages_dev, nodes)
    z, core = tensor_rank // 2, tensor_rank % 2
    far, rest = (z + 2) % 4 * 2, (z + (1 + 2 * jnp.arange(3, dtype=jnp.int32)) % 5) % 4 * 2
    far = jnp.stack([far + 1 - core, far + core])
    other, same = rest + 1 - core, rest + core

    attn, w_held = attend(at, lengths, above, queries, fresh_kv, keys, values, w_out)

    swap = [(t, t ^ 1) for t in range(tensors)]
    cols = D // tensors
    mine = lax.dynamic_slice_in_dim(residual, tensor_rank * cols, cols, 1)
    group = rows // GROUPS
    both = project(far, attn, w_held)
    both, attn = lax.optimization_barrier((both, attn))
    far_back = lax.ppermute(both[0], "tensor", swap)
    away = project(other, attn, w_held)
    far_back, away, attn = lax.optimization_barrier((far_back, away, attn))
    back = lax.ppermute(away, "tensor", swap)
    halves = [((group // 2, cols), jnp.bfloat16)] * (2 * GROUPS)
    sent = local(far_kernel, "far", halves, both, far_back)
    *sent, attn = lax.optimization_barrier((*sent, attn))
    low = [lax.ppermute(sent[2 * g], "tensor", turn(1)) for g in range(GROUPS)]
    high = [lax.ppermute(sent[2 * g + 1], "tensor", turn(-1)) for g in range(GROUPS)]
    kept = project(same, attn, w_held)
    whole = pltpu.VMEM((group, cols), jnp.bfloat16)
    ups, downs = [], []
    for g in range(GROUPS):
        up, down = local(
            functools.partial(near_kernel, g * group), "near", [whole, whole], kept, back, low[g], high[g]
        )
        ups.append(lax.ppermute(up, "tensor", turn(1)))
        downs.append(lax.ppermute(down, "tensor", turn(-1)))
    done = [last(g, kept, back, ups[g], downs[g], mine) for g in range(GROUPS)]

    mixed = jnp.concatenate([m for m, _ in done], axis=0)
    power = jnp.concatenate([p for _, p in done], axis=1)
    for flip in (1, 2, 6):
        power = power + lax.ppermute(power, "tensor", [(t, t ^ flip) for t in range(tensors)])
    norm = lax.rsqrt(power[0].reshape(rows, 1) / D + 1e-05)
    own_gain = lax.dynamic_slice_in_dim(gain, tensor_rank * cols, cols)
    normed = mixed * norm * own_gain.astype(jnp.float32)
    return (mixed.astype(jnp.bfloat16), normed.astype(jnp.bfloat16))


def solution(mesh):
    return jax.shard_map(
        body,
        mesh=mesh,
        in_specs=(
            P("dp", "tensor"),
            P("dp", "tensor"),
            P("dp", None, "tensor"),
            P(),
            P(),
            P(),
            P("tensor", None),
            P("dp", None),
            P(),
        ),
        out_specs=(P("dp", "tensor"), P("dp", "tensor")),
        check_vma=False,
    )
```

```python
import functools

import jax
import jax.numpy as jnp
from jax import lax
from jax.experimental import pallas as pl
from jax.experimental.pallas import tpu as pltpu
from jax.sharding import PartitionSpec as P

D = 8192
HD = 128
NEW = 16
PAGE = 64
PATH_PAGES = 16
SHARED = 8
FAM = 4
RANKS = 16
PAIR = 15
ROOTS = 12
EXTRA = 3
CHUNK = 6
NEAR = (0, 1, 3)
GROUPS = 2
LOG2E = 1.4426950408889634
MIB = 1024 * 1024


def split_kernel(pool_ref, fresh_ref, *refs):
    outs, sem = refs[:-1], refs[-1]
    pages_dev = pool_ref.shape[0]
    for i, out in enumerate(outs):
        lanes = pl.ds(i * HD, HD)
        for start in range(0, pages_dev, CHUNK):
            some = pl.ds(start, min(CHUNK, pages_dev - start))
            pltpu.make_async_copy(pool_ref.at[some, :, lanes], out.at[some], sem.at[i]).start()
        for p in range(EXTRA):
            rows = pl.ds(p * PAGE, PAGE)
            pltpu.make_async_copy(fresh_ref.at[rows, lanes], out.at[pages_dev + p], sem.at[i]).start()
    for i, out in enumerate(outs):
        pltpu.make_async_copy(out, out, sem.at[i]).wait()


def split(pool, fresh):
    hbm = pl.BlockSpec(memory_space=pltpu.HBM)
    vmem = pl.BlockSpec(memory_space=pltpu.VMEM)
    part = pltpu.VMEM((pool.shape[0] + EXTRA, PAGE, HD), pool.dtype)
    return pl.pallas_call(
        split_kernel,
        out_shape=[part, part],
        in_specs=[hbm, hbm],
        out_specs=[vmem, vmem],
        scratch_shapes=[pltpu.SemaphoreType.DMA((2,))],
        compiler_params=pltpu.CompilerParams(vmem_limit_bytes=61 * MIB),
        name="split",
    )(pool, fresh)


def plan_kernel(pages_dev, rank_ref, table_ref, wanted_ref):
    rank = rank_ref[0]
    y, x = rank // 4, rank % 4
    slots, nodes = table_ref.shape
    table = table_ref[...]
    height = -(-pages_dev // 16) * 16
    per_rank = nodes // RANKS
    row = lax.broadcasted_iota(jnp.int32, (height, nodes), 0)
    node = lax.broadcasted_iota(jnp.int32, (nodes, 128), 0)
    column = lax.broadcasted_iota(jnp.int32, (nodes, 128), 1)
    step = column & 3
    begin = jnp.where(column < 16, ((y + step) & 3) * 4 + x, y * 4 + ((x + step) & 3)) * per_rank
    belongs = (node >= begin) & (node < begin + per_rank)
    low = lax.broadcasted_iota(jnp.int32, (height, height), 0)
    high = lax.broadcasted_iota(jnp.int32, (height, height), 1)
    earlier = (high < low).astype(jnp.bfloat16)
    page_id = lax.broadcasted_iota(jnp.int32, (height, 128), 0).astype(jnp.float32)
    line = lax.broadcasted_iota(jnp.int32, (16, 128), 0)
    wanted_ref[...] = jnp.zeros((16, 128), jnp.int32)

    @pl.loop(0, 8)
    def _(part):
        back = part % 4
        owner = jnp.where(part < 4, y * 4 + (x + 4 - back) % 4, (y + 4 - back) % 4 * 4 + x)
        base = owner * pages_dev
        hits = jnp.zeros((height, nodes), jnp.float32)
        for page in range(pages_dev):
            hit = jnp.max((table == base + page).astype(jnp.float32), axis=0, keepdims=True)
            hits = jnp.where(row == page, hit, hits)
        mine = (belongs & (column // 4 == part)).astype(jnp.bfloat16)
        present = jnp.dot(hits.astype(jnp.bfloat16), mine, preferred_element_type=jnp.float32) > 0
        before = jnp.dot(earlier, present.astype(jnp.bfloat16), preferred_element_type=jnp.float32)
        place = jnp.where(present, before, -1.0)
        wanted = jnp.zeros((16, 128), jnp.float32)
        for slot in range(PAIR):
            page = jnp.sum(jnp.where(place == slot, page_id, 0.0), axis=0, keepdims=True)
            wanted = jnp.where(line == slot, page, wanted)
        wanted_ref[...] += wanted.astype(jnp.int32)


def plan(rank, table, pages_dev):
    vmem = pl.BlockSpec(memory_space=pltpu.VMEM)
    return pl.pallas_call(
        functools.partial(plan_kernel, pages_dev),
        out_shape=jax.ShapeDtypeStruct((16, 128), jnp.int32),
        in_specs=[pl.BlockSpec(memory_space=pltpu.SMEM), vmem],
        out_specs=vmem,
        name="plan",
    )(rank, table)


def copy_pages(out, first, ref, wanted_ref, column, pages_dev):
    for slot in range(PAIR):
        page = jnp.clip(wanted_ref[slot, column], 0, pages_dev - 1)
        out[first + slot] = ref[page]


def pack_first_kernel(pages_dev, wanted_ref, *refs):
    sources, outs, (held, stage, in_sems, out_sem) = refs[:6], refs[6:14], refs[14:]
    near = len(NEAR)
    copies = [pltpu.make_async_copy(ref, held.at[k], in_sems.at[k]) for k, ref in enumerate(sources)]
    for copy in copies:
        copy.start()
    for i in range(2):
        for copy in copies[i * near : (i + 1) * near]:
            copy.wait()
        for e in (1, 3, 2, 0):
            part = stage.at[4 * i + e]
            for j, d in enumerate(NEAR):
                copy_pages(part, j * PAIR, held.at[i * near + j], wanted_ref, 16 * i + 4 * d + e, pages_dev)
            pltpu.make_async_copy(part, outs[4 * i + e], out_sem.at[4 * i + e]).start()
    for k, out in enumerate(outs):
        pltpu.make_async_copy(stage.at[k], out, out_sem.at[k]).wait()


def pack_first(wanted, pages_dev, keys, values):
    args = [keys[d] for d in NEAR] + [values[d] for d in NEAR]
    part = (len(NEAR) * PAIR, PAGE, HD)
    scratch = [pltpu.VMEM((len(args),) + keys[0].shape, jnp.bfloat16), pltpu.VMEM((8,) + part, jnp.bfloat16)]
    scratch += [pltpu.SemaphoreType.DMA((len(args),)), pltpu.SemaphoreType.DMA((8,))]
    return packing(functools.partial(pack_first_kernel, pages_dev), "pack_first", part, scratch, [wanted], args)


def packing(kernel, name, part, scratch, scalars, args):
    hbm = pl.BlockSpec(memory_space=pltpu.HBM)
    return pl.pallas_call(
        kernel,
        out_shape=[jax.ShapeDtypeStruct(part, jnp.bfloat16)] * 8,
        in_specs=[pl.BlockSpec(memory_space=pltpu.SMEM)] * len(scalars) + [hbm] * len(args),
        out_specs=[hbm] * 8,
        scratch_shapes=scratch,
        compiler_params=pltpu.CompilerParams(vmem_limit_bytes=59 * MIB),
        name=name,
    )(*scalars, *args)


def pack_second_kernel(pages_dev, rank_ref, parent_ref, wanted_ref, *refs):
    sources, outs, (far, roots, stage, in_sems, out_sem) = refs[:8], refs[8:16], refs[16:]
    y, x = rank_ref[0] // 4, rank_ref[0] % 4
    per_rank = parent_ref.shape[0] // RANKS
    copies = [
        pltpu.make_async_copy(ref.at[pl.ds(pages_dev, EXTRA)], roots.at[k], in_sems.at[k]) for k, ref in enumerate(sources)
    ]
    copies += [pltpu.make_async_copy(sources[4 * i + 2], far.at[i], in_sems.at[8 + i]) for i in range(2)]
    for copy in copies:
        copy.start()
    for copy in copies:
        copy.wait()
    for i in range(2):
        for e in (1, 3, 2, 0):
            part = stage.at[4 * i + e]
            copy_pages(part, 0, far.at[i], wanted_ref, 16 * i + 8 + e, pages_dev)
            dest = (y + e) % 4 * 4 + x if i == 0 else y * 4 + (x + e) % 4
            for child in range(per_rank - ROOTS):
                named = jnp.maximum(parent_ref[dest * per_rank + ROOTS + child], 0)
                up = named // per_rank
                away = (x + 4 - up % 4) % 4 if i == 0 else (y + 4 - up // 4) % 4
                root = jnp.minimum(named % per_rank, ROOTS - 1)
                rows = pl.ds(pl.multiple_of(root % 4 * NEW, NEW), NEW)
                part[PAIR + child // 4, child % 4 * NEW : (child % 4 + 1) * NEW, :] = roots[4 * i + away, root // 4, rows, :]
            pltpu.make_async_copy(part, outs[4 * i + e], out_sem.at[4 * i + e]).start()
    for k, out in enumerate(outs):
        pltpu.make_async_copy(stage.at[k], out, out_sem.at[k]).wait()


def pack_second(rank, parent, wanted, pages_dev, keys, values):
    part = (PAIR + EXTRA, PAGE, HD)
    scratch = [
        pltpu.VMEM((2,) + keys[0].shape, jnp.bfloat16),
        pltpu.VMEM((8, EXTRA, PAGE, HD), jnp.bfloat16),
        pltpu.VMEM((8,) + part, jnp.bfloat16),
        pltpu.SemaphoreType.DMA((10,)),
        pltpu.SemaphoreType.DMA((8,)),
    ]
    kernel = functools.partial(pack_second_kernel, pages_dev)
    return packing(kernel, "pack_second", part, scratch, [rank, parent, wanted], [*keys, *values])


def attend_family(wait_values, first, node, at_refs, len_ref, above_refs, q_ref, fresh_ref, page_refs, attn_ref):
    scale = HD ** (-0.5) * LOG2E
    nt = (((1,), (1,)), ((), ()))

    def pages(i, n, slot):
        return [page_refs[i][at_refs[i][n * PATH_PAGES + slot + s]] for s in range(SHARED)]

    heads = q_ref.shape[1] // HD
    span = heads * NEW
    shared_key = jnp.concatenate(pages(0, node, 0), axis=0)
    queries = []
    for i in range(FAM):
        rows = q_ref[first + i * NEW : first + (i + 1) * NEW, :]
        queries.append(jnp.concatenate([rows[:, h * HD : (h + 1) * HD] for h in range(heads)], axis=0))
    s_shared = lax.dot_general(
        jnp.concatenate(queries, axis=0), shared_key, nt, preferred_element_type=jnp.float32
    )
    half = SHARED * PAGE // 2
    def near(j, i):
        spot = jnp.maximum(above_refs[j][node + i], 0)
        upper = page_refs[j][spot // PAGE, pl.ds(pl.multiple_of(spot % PAGE, NEW), NEW), :]
        fresh = fresh_ref[first + i * NEW : first + (i + 1) * NEW, j * HD : (j + 1) * HD]
        return jnp.concatenate(pages(j, node + i, SHARED) + [fresh, upper], axis=0)

    s_own = []
    for i in range(FAM):
        s = lax.dot_general(queries[i], near(0, i), nt, preferred_element_type=jnp.float32)
        late = s[:, half:]
        spot = lax.broadcasted_iota(jnp.int32, late.shape, 1) + SHARED * PAGE + half
        token = lax.broadcasted_iota(jnp.int32, late.shape, 0) % NEW
        key = spot - PATH_PAGES * PAGE
        limit = jnp.where(above_refs[0][node + i] >= 0, 2 * NEW, NEW)
        allowed = (spot < len_ref[node + i]) | ((key >= 0) & (key <= token)) | ((key >= NEW) & (key < limit))
        s_own.append(jnp.concatenate([s[:, :half], jnp.where(allowed, late, -jnp.inf)], axis=1))
    tops = [
        jnp.maximum(
            jnp.max(s_shared[i * span : (i + 1) * span], axis=1, keepdims=True),
            jnp.max(s_own[i], axis=1, keepdims=True),
        )
        for i in range(FAM)
    ]
    w_own = [jnp.exp2((s_own[i] - tops[i]) * scale).astype(jnp.bfloat16) for i in range(FAM)]
    w_shared = jnp.exp2((s_shared - jnp.concatenate(tops, axis=0)) * scale).astype(jnp.bfloat16)
    wait_values()
    values = [near(1, i) for i in range(FAM)]
    shared_value = jnp.concatenate(pages(1, node, 0), axis=0)
    ones = jnp.ones((values[0].shape[0], HD), jnp.bfloat16)
    accum = [
        jnp.dot(w_own[i], jnp.concatenate([values[i], ones], axis=1), preferred_element_type=jnp.float32)
        for i in range(FAM)
    ]
    accum = jnp.concatenate(accum, axis=0) + jnp.dot(
        w_shared, jnp.concatenate([shared_value, ones[: SHARED * PAGE]], axis=1), preferred_element_type=jnp.float32
    )
    attn = (accum[:, :HD] / accum[:, HD:]).astype(jnp.bfloat16)
    for i in range(FAM):
        for h in range(heads):
            block = attn[i * span + h * NEW : i * span + (h + 1) * NEW, :]
            attn_ref[first + i * NEW : first + (i + 1) * NEW, h * HD : (h + 1) * HD] = block


def attend_kernel(*refs):
    at_refs, len_ref, above_refs, (q_ref, fresh_ref) = refs[:2], refs[2], refs[3:5], refs[5:7]
    sources, w_hbm, (attn_ref, w_ref), page_refs, sems = (refs[7:15], refs[15:23]), refs[23], refs[24:26], refs[26:28], refs[28]
    for i in range(2):
        start = 0
        for ref in sources[i]:
            count = ref.shape[0]
            pltpu.make_async_copy(ref, page_refs[i].at[pl.ds(start, count)], sems.at[i]).start()
            start += count
    weights = []
    for part in range(8):
        rows = pl.ds(part * (w_ref.shape[0] // 8), w_ref.shape[0] // 8)
        weights.append(pltpu.make_async_copy(w_hbm.at[rows], w_ref.at[rows], sems.at[2 + part]))
        weights[-1].start()
    all_pages = [pltpu.make_async_copy(page_refs[i], page_refs[i], sems.at[i]) for i in range(2)]
    all_pages[0].wait()
    for f in range(q_ref.shape[0] // (FAM * NEW)):
        wait_values = all_pages[1].wait if f == 0 else lambda: None
        attend_family(
            wait_values, f * FAM * NEW, f * FAM, at_refs, len_ref, above_refs, q_ref, fresh_ref, page_refs, attn_ref
        )
    for copy in weights:
        copy.wait()


def attend(at, lengths, above, queries, fresh, keys, values, w_out):
    rows, width = queries.shape
    smem = pl.BlockSpec(memory_space=pltpu.SMEM)
    vmem = pl.BlockSpec(memory_space=pltpu.VMEM)
    hbm = pl.BlockSpec(memory_space=pltpu.HBM)
    pages = pltpu.VMEM((sum(k.shape[0] for k in keys), PAGE, HD), jnp.bfloat16)
    return pl.pallas_call(
        attend_kernel,
        out_shape=[pltpu.VMEM((rows, width), jnp.bfloat16), pltpu.VMEM(w_out.shape, w_out.dtype)],
        in_specs=[smem] * 5 + [vmem] * 2 + [hbm] * 17,
        out_specs=[vmem, vmem],
        scratch_shapes=[pages, pages, pltpu.SemaphoreType.DMA((10,))],
        compiler_params=pltpu.CompilerParams(vmem_limit_bytes=44 * MIB),
        cost_estimate=pl.CostEstimate(
            flops=4 * rows * width * 1056 * 4, bytes_accessed=4 * rows * width, transcendentals=rows * 8 * 1056
        ),
        name="attend",
    )(*at, lengths, *above, queries, fresh, *keys, *values, w_out)


def project_kernel(order_ref, attn_ref, w_ref, out_ref):
    count, rows, cols = out_ref.shape

    @pl.loop(0, count)
    def _(b):
        w = w_ref[:, pl.ds(pl.multiple_of(order_ref[b] * cols, cols), cols)]
        out_ref[b] = jnp.dot(attn_ref[...], w, preferred_element_type=jnp.float32).astype(jnp.bfloat16)


def project(order, attn, w_out):
    rows, depth = attn.shape
    cols = w_out.shape[1] // 8
    count = order.shape[0]
    smem = pl.BlockSpec(memory_space=pltpu.SMEM)
    vmem = pl.BlockSpec(memory_space=pltpu.VMEM)
    return pl.pallas_call(
        project_kernel,
        out_shape=jax.ShapeDtypeStruct((count, rows, cols), jnp.bfloat16),
        in_specs=[smem, vmem, vmem],
        out_specs=vmem,
        compiler_params=pltpu.CompilerParams(vmem_limit_bytes=12 * MIB),
        cost_estimate=pl.CostEstimate(
            flops=2 * rows * depth * cols * count, bytes_accessed=rows * cols * count * 2, transcendentals=0
        ),
        name="project",
    )(order, attn, w_out)


def shift(dy, dx):
    return [(s, (s // 4 + dy) % 4 * 4 + (s % 4 + dx) % 4) for s in range(RANKS)]


def turn(d):
    return [(t, (t + 2 * d) % 8) for t in range(8)]


def places_of(table, path_parent, rank, pages_dev, nodes):
    owner = table // pages_dev
    other, mine = table[None, :], table[:, None]
    slot = jnp.arange(table.shape[0], dtype=jnp.int32)
    first = (slot % PATH_PAGES >= SHARED) | (slot // PATH_PAGES % FAM == 0)
    before = (other < mine) & (other >= (owner * pages_dev)[:, None]) & first[None, :]
    place = jnp.sum(before.astype(jnp.int32), axis=1)
    child = jnp.arange(nodes, dtype=jnp.int32) - ROOTS
    up = jnp.maximum(path_parent, 0) // nodes
    many, few = len(NEAR) * PAIR, PAIR + EXTRA

    def turns(r):
        return (rank // 4 - r // 4) % 4, (rank % 4 - r % 4) % 4

    at, above = [], []
    for i in range(2):
        e, d = turns(owner)[:: 1 - 2 * i]
        at.append(jnp.where(d == 2, 4 * many + e * few, e * many + jnp.minimum(d, 2) * PAIR) + place)
        row = (4 * many + turns(up)[i] * few + PAIR) * PAGE + child * NEW
        above.append(jnp.where((path_parent >= 0) & (child >= 0), row, -1))
    return at, above


def far_kernel(kept_ref, back_ref, *out_refs):
    rows = out_refs[0].shape[0]
    for i, ref in enumerate(out_refs):
        part = pl.ds(i * rows, rows)
        ref[...] = (kept_ref[1, part].astype(jnp.float32) + back_ref[part].astype(jnp.float32)).astype(jnp.bfloat16)


def near_kernel(first, kept_ref, back_ref, from_low_ref, from_high_ref, up_ref, down_ref):
    half = from_low_ref.shape[0]
    low, high = pl.ds(0, half), pl.ds(half, half)

    def pair(i, start):
        part = pl.ds(first + start, half)
        return kept_ref[i, part].astype(jnp.float32) + back_ref[i, part].astype(jnp.float32)

    up_ref[low] = (pair(0, 0) + from_low_ref[...].astype(jnp.float32)).astype(jnp.bfloat16)
    up_ref[high] = pair(0, half).astype(jnp.bfloat16)
    down_ref[low] = pair(1, 0).astype(jnp.bfloat16)
    down_ref[high] = (pair(1, half) + from_high_ref[...].astype(jnp.float32)).astype(jnp.bfloat16)


def last_kernel(kept_ref, back_ref, up_ref, down_ref, residual_ref, mixed_ref, power_ref):
    mixed = residual_ref[...].astype(jnp.float32)
    for term in (kept_ref[0], back_ref[0], up_ref[...], down_ref[...]):
        mixed = mixed + term.astype(jnp.float32)
    mixed_ref[...] = mixed
    squares = mixed * mixed
    power_ref[...] = lax.dot_general(
        jnp.ones((8, 128), jnp.float32),
        sum(squares[:, start : start + 128] for start in range(0, mixed.shape[1], 128)),
        (((1,), (1,)), ((), ())),
        precision=lax.Precision.HIGHEST,
        preferred_element_type=jnp.float32,
    )


def last(g, kept, back, up, down, residual):
    group, cols = up.shape
    own = pl.BlockSpec((1, group, cols), lambda i: (2, g, 0))
    whole = pl.BlockSpec((group, cols), lambda i: (0, 0))
    return pl.pallas_call(
        last_kernel,
        out_shape=[jax.ShapeDtypeStruct((group, cols), jnp.float32), jax.ShapeDtypeStruct((8, group), jnp.float32)],
        grid=(1,),
        in_specs=[own, own, whole, whole, pl.BlockSpec((group, cols), lambda i: (g, 0))],
        out_specs=[whole, pl.BlockSpec((8, group), lambda i: (0, 0))],
        compiler_params=pltpu.CompilerParams(vmem_limit_bytes=12 * MIB),
        name="last",
    )(kept, back, up, down, residual)


def local(kernel, name, outs, *args, scalars=0, limit=12):
    vmem = pl.BlockSpec(memory_space=pltpu.VMEM)
    smem = pl.BlockSpec(memory_space=pltpu.SMEM)
    return pl.pallas_call(
        kernel,
        out_shape=[jax.ShapeDtypeStruct(*out) if isinstance(out, tuple) else out for out in outs],
        in_specs=[smem] * scalars + [vmem] * (len(args) - scalars),
        out_specs=[vmem] * len(outs),
        compiler_params=pltpu.CompilerParams(vmem_limit_bytes=limit * MIB),
        name=name,
    )(*args)


def body(queries, fresh_kv, kv_pool, page_table, path_len, parent, w_out, residual, gain):
    rank = lax.axis_index("dp")
    tensor_rank = lax.axis_index("tensor")
    tensors = lax.axis_size("tensor")
    rows = queries.shape[0]
    nodes = rows // NEW
    pages_dev = kv_pool.shape[0]
    key, value = split(kv_pool, fresh_kv)
    place = rank.reshape(1)
    wanted = plan(place, page_table.T, pages_dev)
    far_key, far_value, wanted = lax.optimization_barrier((key, value, wanted))
    keys = [key] + [lax.ppermute(far_key if d == 2 else key, "dp", shift(0, d)) for d in (1, 2, 3)]
    values = [value] + [lax.ppermute(far_value if d == 2 else value, "dp", shift(d, 0)) for d in (1, 2, 3)]
    first = list(pack_first(wanted, pages_dev, keys, values))

    def deliver(parts):
        order = [(e, i) for e in (1, 3, 2) for i in range(2)]
        return {(i, e): lax.ppermute(parts[4 * i + e], "dp", shift(0, e) if i else shift(e, 0)) for e, i in order}

    got = deliver(first)
    got[0, 1], wanted = lax.optimization_barrier((got[0, 1], wanted))
    second = list(pack_second(place, parent, wanted, pages_dev, keys, values))
    for i, e in got:
        if (i, e) != (0, 1):
            got[i, e], second[4 * i + e] = lax.optimization_barrier((got[i, e], second[4 * i + e]))
    more = deliver(second)
    keys, values = (
        [first[4 * i]] + [got[i, e] for e in (1, 2, 3)] + [second[4 * i]] + [more[i, e] for e in (1, 2, 3)]
        for i in range(2)
    )
    keys, values, w_out, residual, gain = lax.optimization_barrier((keys, values, w_out, residual, gain))

    own_table = lax.dynamic_slice_in_dim(page_table, rank * nodes, nodes).reshape(-1)
    lengths = lax.dynamic_slice_in_dim(path_len, rank * nodes, nodes)
    at, above = places_of(own_table, lax.dynamic_slice_in_dim(parent, rank * nodes, nodes), rank, pages_dev, nodes)
    z, core = tensor_rank // 2, tensor_rank % 2
    far, rest = (z + 2) % 4 * 2, (z + (1 + 2 * jnp.arange(3, dtype=jnp.int32)) % 5) % 4 * 2
    far = jnp.stack([far + 1 - core, far + core])
    other, same = rest + 1 - core, rest + core

    attn, w_held = attend(at, lengths, above, queries, fresh_kv, keys, values, w_out)

    swap = [(t, t ^ 1) for t in range(tensors)]
    cols = D // tensors
    mine = lax.dynamic_slice_in_dim(residual, tensor_rank * cols, cols, 1)
    group = rows // GROUPS
    both = project(far, attn, w_held)
    both, attn = lax.optimization_barrier((both, attn))
    far_back = lax.ppermute(both[0], "tensor", swap)
    away = project(other, attn, w_held)
    far_back, away, attn = lax.optimization_barrier((far_back, away, attn))
    back = lax.ppermute(away, "tensor", swap)
    halves = [((group // 2, cols), jnp.bfloat16)] * (2 * GROUPS)
    sent = local(far_kernel, "far", halves, both, far_back)
    *sent, attn = lax.optimization_barrier((*sent, attn))
    low = [lax.ppermute(sent[2 * g], "tensor", turn(1)) for g in range(GROUPS)]
    high = [lax.ppermute(sent[2 * g + 1], "tensor", turn(-1)) for g in range(GROUPS)]
    kept = project(same, attn, w_held)
    whole = pltpu.VMEM((group, cols), jnp.bfloat16)
    ups, downs = [], []
    for g in range(GROUPS):
        up, down = local(
            functools.partial(near_kernel, g * group), "near", [whole, whole], kept, back, low[g], high[g]
        )
        ups.append(lax.ppermute(up, "tensor", turn(1)))
        downs.append(lax.ppermute(down, "tensor", turn(-1)))
    done = [last(g, kept, back, ups[g], downs[g], mine) for g in range(GROUPS)]

    mixed = jnp.concatenate([m for m, _ in done], axis=0)
    power = jnp.concatenate([p for _, p in done], axis=1)
    for flip in (1, 2, 6):
        power = power + lax.ppermute(power, "tensor", [(t, t ^ flip) for t in range(tensors)])
    norm = lax.rsqrt(power[0].reshape(rows, 1) / D + 1e-05)
    own_gain = lax.dynamic_slice_in_dim(gain, tensor_rank * cols, cols)
    normed = mixed * norm * own_gain.astype(jnp.float32)
    return (mixed.astype(jnp.bfloat16), normed.astype(jnp.bfloat16))


def solution(mesh):
    return jax.shard_map(
        body,
        mesh=mesh,
        in_specs=(
            P("dp", "tensor"),
            P("dp", "tensor"),
            P("dp", None, "tensor"),
            P(),
            P(),
            P(),
            P("tensor", None),
            P("dp", None),
            P(),
        ),
        out_specs=(P("dp", "tensor"), P("dp", "tensor")),
        check_vma=False,
    )
```
